32 devices in a mesh: groups: 2 (over y), ep: 8 (over z, x), tp: 2 (over core).
Axes of the slice: x: 2, y: 2, z: 4, core: 2. Of those that a mesh axis runs over, the one named last changes fastest.
Arguments:
- tokens: bfloat16 [1024, 3584], P(('groups', 'ep'), 'tp'), parts along dimension 0, may hold values from -6 to 6
- expert_ids: int32 [1024, 1], P(('groups', 'ep')), parts along dimension 0, may hold values from 0 to 1; in each aligned block of 64 rows (0 to 63, 64 to 127, ...) at most 64 rows name the same one
- gate_fixed: int32 [1024, 1], P(('groups', 'ep')), parts along dimension 0, may hold values from 256 to 4095
- w_gate: bfloat16 [8, 3584, 256], P('ep', None, 'tp'), may hold values from -0.09375 to 0.09375
- w_up: bfloat16 [8, 3584, 256], P('ep', None, 'tp'), may hold values from -0.09375 to 0.09375
- w_down: bfloat16 [8, 256, 3584], P('ep', 'tp'), may hold values from -0.1875 to 0.1875
Outputs:
- mixed: bfloat16 [1024, 3584], P(('groups', 'ep'), 'tp'), parts along dimension 0
The draws below stay inside these ranges and needn't reach their ends.
There are 2 independent parts, one for each index of `groups`. The reference program is written for one: setup_inputs(seed, part) draws one part's arguments, and reference() takes and returns one part's arrays. A program takes and returns all parts, laid end to end along the dimension named above; an argument that names none is the same for every part. Nothing has to cross between parts.
Inputs may be any that keep to these rules, and one draw needn't show every extreme that they name: `expert_ids`: in each aligned block of 64 tokens no expert is named by more than 64 routes, and in some blocks one is named by exactly 64; a token's ids differ. `gate_fixed`: gate weight times 2048.
All inputs are finite; a program needn't handle non-finite values.
Results may differ from the reference program's by a relative error of at most 0.0066.
Values may be sent and summed in bfloat16 or wider, within the bound.
No kernel may reach another device: no remote copies, remote signals or barrier semaphores. Data moves between devices by JAX's collectives and lax.ppermute only.
A program may use at most 64 MiB of HBM per device.

```python
import math
import jax
import jax.numpy as jnp
import numpy as np
from jax import lax

D = 3584
FF = 1024
ESPLIT = 4
TOPK = 1
TOK_DEV = 64
TOKENS = 512
EXPERTS = 2
CAP = 64
N_EP = 8
N_TP = 2


def place_ends(array, stream_key, least, largest):
    longest = array.shape.index(max(array.shape))
    spots = []
    for shift in (0, 1):
        where = [jax.random.randint(jax.random.fold_in(stream_key, axis), (), 0, length) for axis, length in enumerate(array.shape)]
        where[longest] = (where[longest] + shift) % array.shape[longest]
        spots.append(tuple(where))
    return array.at[spots[0]].set(least).at[spots[1]].set(largest)


def levels(key, shape, pieces, low, high):
    loudness = 1.0
    for dim, parts in pieces:
        steps = jax.random.uniform(jax.random.fold_in(jax.random.fold_in(key, 6), dim), (parts,), jnp.float32, low / len(pieces), high / len(pieces))
        loudness = loudness * jnp.repeat(jnp.exp(steps), shape[dim] // parts).reshape((-1,) + (1,) * (len(shape) - 1 - dim))
    return loudness


def deal_out(key, own, number, rows, number_of, top, bound, skew):
    order = jax.random.permutation(key, number_of)
    crowded, usual = load_shares(number_of, rows * top, bound, skew, True), load_shares(number_of, rows * top, bound, skew, False)
    places = jnp.arange(number_of)

    def named(sizes, turn):
        used = int((sizes > 0).sum())
        fixed = max(1, used // 4)
        passed = fixed + (places - fixed + turn * (used - fixed)) % max(1, number_of - fixed)
        return jnp.zeros((number_of,), jnp.int32).at[order[jnp.where(places < fixed, places, passed)]].set(jnp.asarray(sizes, jnp.int32))

    sizes = jnp.where(number % 4 == 0, named(crowded, number // 4), named(usual, number - number // 4 - 1))
    mixed = jax.random.permutation(jax.random.fold_in(own, 3), number_of)
    source_of, sink = mixed[0:number_of // 2 * 2:2], mixed[1:number_of // 2 * 2:2]
    margin = jnp.minimum(sizes[source_of] - 1, bound - sizes[sink]) // 2
    margin = jnp.where((source_of == order[0]) | (sink == order[0]) | (sizes[sink] == 0), 0, jnp.maximum(margin, 0))
    passed = jax.random.randint(jax.random.fold_in(own, 4), (number_of // 2,), 0, 1 << 20) % (margin + 1)
    sizes = sizes.at[source_of].add(-passed).at[sink].add(passed)
    members = jnp.searchsorted(jnp.cumsum(sizes), jnp.arange(rows * top), side="right").astype(jnp.int32)
    listing = members.reshape(top, rows).T
    listing = listing[jax.random.permutation(jax.random.fold_in(own, 1), rows)]
    turn = jax.random.randint(jax.random.fold_in(own, 2), (rows, 1), 0, top)
    return jnp.take_along_axis(listing, (jnp.arange(top)[None, :] + turn) % top, axis=1)


def load_shares(amount, total, most, lean, full):
    portions = [(1 << 20) // math.isqrt(rank ** lean) + 1 for rank in range(1, amount + 1)]
    largest = most if full else min(most, max(-(-total // amount), total * portions[0] // sum(portions)))
    least = 1 if total - largest >= amount - 1 else 0
    given, spare = [largest] + [least] * (amount - 1), total - largest - least * (amount - 1)
    while spare > 0:
        movable = [i for i in range(1, amount) if given[i] < largest] or [i for i in range(1, amount) if given[i] < most]
        whole, remaining = sum([portions[i] for i in movable]), spare
        for i in movable:
            addition = min(most - given[i], max(1, remaining * portions[i] // whole), spare)
            given[i] = given[i] + addition
            spare = spare - addition
    return np.array(given)


def normal_values(key, dims, deviation, limit, shards=(), held_as=jnp.bfloat16):
    factor_of = levels(key, dims, shards, -0.22, 0.18) if shards else 1.0
    result = jax.random.normal(key, dims, jnp.float32) * deviation * factor_of
    return jnp.minimum(jnp.maximum(result, -limit), limit).astype(held_as)


def setup_inputs(seed: int = 0, part: int = 0) -> dict:
    keys = jax.random.split(jax.random.key(seed), 7)
    part_splits = jax.random.split(jax.random.fold_in(keys[6], part), 7)
    tokens = normal_values(part_splits[0], (TOKENS, D), 1.0, 6.0, ((0, 8), (1, 2)))
    expert_ids_keys = jax.random.split(jax.random.fold_in(part_splits[1], 1), TOKENS // TOK_DEV)
    expert_ids_turns = jax.random.permutation(jax.random.fold_in(part_splits[1], 3), TOKENS // TOK_DEV)
    expert_ids = jax.vmap(lambda own, number: deal_out(jax.random.fold_in(part_splits[1], 2), own, number, TOK_DEV, EXPERTS, TOPK, CAP, 2))(expert_ids_keys, expert_ids_turns).reshape((TOKENS, TOPK))
    gate_fixed = place_ends(jax.random.randint(part_splits[2], (TOKENS, TOPK), 256, 4096), jax.random.fold_in(part_splits[2], 1), 256, 4095).astype(jnp.int32)
    w_gate = normal_values(keys[3], (EXPERTS * ESPLIT, D, FF // ESPLIT), D ** -0.5, 0.09375, ((0, 8), (2, 2)))
    w_up = normal_values(keys[4], (EXPERTS * ESPLIT, D, FF // ESPLIT), D ** -0.5, 0.09375, ((0, 8), (2, 2)))
    w_down = normal_values(keys[5], (EXPERTS * ESPLIT, FF // ESPLIT, D), FF ** -0.5, 0.1875, ((0, 8), (1, 2)))
    return dict(tokens=tokens, expert_ids=expert_ids, gate_fixed=gate_fixed, w_gate=w_gate, w_up=w_up, w_down=w_down)


def expert_output(rows, w_gate, w_up, w_down, expert_index):
    units = FF // ESPLIT // N_TP
    total = jnp.zeros((rows.shape[0], D), jnp.float32)
    for quarter in range(ESPLIT):
        row_index = expert_index * ESPLIT + quarter
        gate_weight = lax.dynamic_index_in_dim(w_gate, row_index, 0, keepdims=False)
        up_weight = lax.dynamic_index_in_dim(w_up, row_index, 0, keepdims=False)
        down_weight = lax.dynamic_index_in_dim(w_down, row_index, 0, keepdims=False)
        gate_act = jnp.dot(rows, gate_weight, preferred_element_type=jnp.float32)
        up_act = jnp.dot(rows, up_weight, preferred_element_type=jnp.float32)
        hidden = (jax.nn.silu(gate_act) * up_act).astype(jnp.bfloat16)
        quarter_sum = jnp.zeros((rows.shape[0], D), jnp.float32)
        for slice_index in range(N_TP):
            piece = jnp.dot(hidden[:, slice_index * units:(slice_index + 1) * units],
                            down_weight[slice_index * units:(slice_index + 1) * units],
                            preferred_element_type=jnp.float32).astype(jnp.bfloat16)
            piece = lax.optimization_barrier(piece)
            quarter_sum = quarter_sum + piece.astype(jnp.float32)
        quarter_low = lax.optimization_barrier(quarter_sum.astype(jnp.bfloat16))
        total = total + quarter_low.astype(jnp.float32)
    return total


def reference(tokens, expert_ids, gate_fixed, w_gate, w_up, w_down):
    route_count = TOK_DEV * TOPK
    block_ids = expert_ids.reshape(N_EP, route_count)
    position = jnp.arange(route_count)
    earlier = position[:, None] < position[None, :]
    matches = (block_ids[:, :, None] == block_ids[:, None, :]) & earlier[None]
    ranks = jnp.sum(matches, axis=1).astype(jnp.int32)
    source = jnp.arange(N_EP, dtype=jnp.int32)[:, None]
    slot_index = (block_ids * (N_EP * CAP) + source * CAP + ranks).reshape(-1)
    token_of = (jnp.arange(TOKENS * TOPK, dtype=jnp.int32) // TOPK).astype(jnp.int32)
    table = jnp.zeros((EXPERTS * N_EP * CAP,), jnp.int32).at[slot_index].set(token_of)
    table = table.reshape(EXPERTS, N_EP * CAP)

    def one_expert(expert_index):
        rows = tokens[lax.dynamic_index_in_dim(table, expert_index, 0, keepdims=False)]
        return expert_output(rows, w_gate, w_up, w_down, expert_index)

    outputs = lax.map(one_expert, jnp.arange(EXPERTS, dtype=jnp.int32))
    routed = outputs.reshape(EXPERTS * N_EP * CAP, D)[slot_index]
    weights_route = gate_fixed.reshape(-1).astype(jnp.float32) / 2048.0
    routed = routed * weights_route[:, None]
    return jnp.sum(routed.reshape(TOKENS, TOPK, D), axis=1).astype(jnp.bfloat16)
```

```python
import jax
import jax.numpy as jnp
from jax import lax
from jax.sharding import PartitionSpec as P

ESPLIT = 4


def earlier_ranks(labels):
    position = jnp.arange(labels.shape[0])
    matches = (labels[:, None] == labels[None, :]) & (position[:, None] < position[None, :])
    return jnp.sum(matches, axis=0)


def swap(value, bit):
    pairs = [(i, i ^ bit) for i in range(lax.axis_size("ep"))]
    return lax.ppermute(value, "ep", pairs)


def swap_core(value):
    return lax.ppermute(value, "tp", [(0, 1), (1, 0)])


def dense_body(tokens, expert_ids, gate_fixed, w_gate, w_up, w_down):
    core = lax.axis_index("tp")
    first = core == 0
    half = tokens.shape[0] // 2
    top, bottom = tokens[:half], tokens[half:]
    mine = jnp.where(first, top, bottom)
    theirs = swap_core(jnp.where(first, bottom, top))
    block = jnp.concatenate(
        [jnp.where(first, mine, theirs), jnp.where(first, theirs, mine)], axis=1
    )
    w_gate, w_up, w_down = w_gate[0], w_up[0], w_down[0]
    weights = [(w_gate, w_up, w_down), (swap_core(w_gate), swap_core(w_up), swap_core(w_down))]

    held = {0: block}
    held[4] = swap(block, 4)
    held[2] = swap(block, 2)
    held[1] = swap(block, 1)
    held[6] = swap(held[4], 2)
    for m in (2, 4, 6):
        held[m | 1] = swap(held[m], 1)

    def expert(m):
        rows = jnp.concatenate([held[m], held[m | 1]], axis=0)
        out = None
        for gate, up, down in weights:
            gate_act = jnp.dot(rows, gate, preferred_element_type=jnp.float32)
            up_act = jnp.dot(rows, up, preferred_element_type=jnp.float32)
            hidden = (jax.nn.silu(gate_act) * up_act).astype(jnp.bfloat16)
            part = jnp.dot(hidden, down, preferred_element_type=jnp.float32)
            out = part if out is None else out + part
        return out[:half], out[half:].astype(jnp.bfloat16)

    pair = {}
    for m in (6, 4, 2, 0):
        own, sent = expert(m)
        pair[m] = own + swap(sent, 1).astype(jnp.float32)
    far = pair[4] + swap(pair[6].astype(jnp.bfloat16), 2).astype(jnp.float32)
    near = pair[0] + swap(pair[2].astype(jnp.bfloat16), 2).astype(jnp.float32)
    other = swap(far.astype(jnp.bfloat16), 4).astype(jnp.float32)

    ids = lax.dynamic_slice_in_dim(expert_ids, core * half, half, 0)
    scale = lax.dynamic_slice_in_dim(gate_fixed, core * half, half, 0).astype(jnp.float32) / 2048.0
    here = lax.axis_index("ep") // ESPLIT
    mixed = (jnp.where(ids == here, near, other) * scale).astype(jnp.bfloat16)
    width = tokens.shape[1]
    left, right = mixed[:, :width], mixed[:, width:]
    keep = jnp.where(first, left, right)
    got = swap_core(jnp.where(first, right, left))
    return jnp.concatenate([jnp.where(first, keep, got), jnp.where(first, got, keep)], axis=0)


def routed_body(tokens, expert_ids, gate_fixed, w_gate, w_up, w_down):
    ep_count = lax.axis_size("ep")
    tok_dev, topk = expert_ids.shape
    experts = ep_count // ESPLIT
    capacity = max(2, min(tok_dev, 2 * tok_dev * topk // experts))
    flat_ids = expert_ids.reshape(-1)
    slot_index = flat_ids * capacity + earlier_ranks(flat_ids)
    chooser = (slot_index[None, :] == jnp.arange(experts * capacity)[:, None]).astype(jnp.bfloat16)
    whole = lax.all_gather(tokens, "tp", axis=1, tiled=True)
    width = whole.shape[1]
    routed_rows = jnp.repeat(whole, topk, axis=0)
    grouped = jnp.dot(chooser, routed_rows, preferred_element_type=jnp.float32).astype(jnp.bfloat16)
    grouped = grouped.reshape(experts, 1, capacity, width)
    copies = jnp.broadcast_to(grouped, (experts, ESPLIT, capacity, width))
    arrived = lax.all_to_all(
        copies.reshape(ep_count, capacity, width), "ep", split_axis=0, concat_axis=0, tiled=True
    )
    expert_rows = arrived.reshape(ep_count * capacity, arrived.shape[2])
    gate_act = jnp.dot(expert_rows, w_gate[0], preferred_element_type=jnp.float32)
    up_act = jnp.dot(expert_rows, w_up[0], preferred_element_type=jnp.float32)
    hidden = (jax.nn.silu(gate_act) * up_act).astype(jnp.bfloat16)
    partial_out = jnp.dot(hidden, w_down[0], preferred_element_type=jnp.float32).astype(
        jnp.bfloat16
    )
    summed = (
        lax.psum_scatter(partial_out, "tp", scatter_dimension=1, tiled=True)
        .astype(jnp.float32)
        .astype(jnp.bfloat16)
    )
    returned = lax.all_to_all(
        summed.reshape(ep_count, capacity, summed.shape[1]),
        "ep",
        split_axis=0,
        concat_axis=0,
        tiled=True,
    )
    quarters = jnp.sum(
        returned.reshape(experts, ESPLIT, capacity, returned.shape[2]).astype(jnp.float32), axis=1
    )
    quarters = quarters.reshape(experts * capacity, returned.shape[2])
    weights_route = gate_fixed.reshape(-1).astype(jnp.float32) / 2048.0
    routed = quarters[slot_index] * weights_route[:, None]
    return jnp.sum(routed.reshape(tok_dev, topk, routed.shape[1]), axis=1).astype(jnp.bfloat16)


def body(tokens, expert_ids, *rest):
    experts = lax.axis_size("ep") // ESPLIT
    dense = experts == 2 and expert_ids.shape[1] == 1
    return (dense_body if dense else routed_body)(tokens, expert_ids, *rest)


def solution(mesh):
    placed = (
        P(("groups", "ep"), "tp"),
        P(("groups", "ep"), None),
        P(("groups", "ep"), None),
        P("ep", None, "tp"),
        P("ep", None, "tp"),
        P("ep", "tp", None),
    )
    return jax.shard_map(
        body, mesh=mesh, in_specs=placed, out_specs=P(("groups", "ep"), "tp"), check_vma=False
    )
```

```python
import functools

import jax
import jax.numpy as jnp
from jax import lax
from jax.experimental import pallas as pl
from jax.experimental.pallas import tpu as pltpu
from jax.sharding import PartitionSpec as P

ESPLIT = 4
VMEM = pl.BlockSpec(memory_space=pltpu.VMEM)


def earlier_ranks(labels):
    position = jnp.arange(labels.shape[0])
    matches = (labels[:, None] == labels[None, :]) & (position[:, None] < position[None, :])
    return jnp.sum(matches, axis=0)


def swap(value, bit):
    pairs = [(i, i ^ bit) for i in range(lax.axis_size("ep"))]
    return lax.ppermute(value, "ep", pairs)


def swap_core(value):
    return lax.ppermute(value, "tp", [(0, 1), (1, 0)])


def expert_kernel(count, *refs):
    split, at = [], 0
    for n in (*count[:2], 2, *count[2:]):
        split.append(refs[at : at + n])
        at += n
    near, far, (w_in, w_out), near_out, far_out = split
    first = lax.axis_index("tp") == 0

    def halves(refs):
        return [r[...] for r in refs] if len(refs) == 2 else [refs[0][0], refs[0][1]]

    def run(order):
        rows = jnp.concatenate(
            [jnp.concatenate([halves(near)[i], halves(far)[i]], axis=0) for i in order], axis=1
        )
        act = jnp.dot(rows, w_in[...], preferred_element_type=jnp.float32)
        units = act.shape[1] // 2
        gate, up = act[:, :units], act[:, units:]
        hidden = (gate / (1 + jnp.exp(-gate)) * up).astype(jnp.bfloat16)
        out = jnp.dot(hidden, w_out[...], preferred_element_type=jnp.float32)
        half, width = rows.shape[0] // 2, rows.shape[1] // 2
        for place, i in enumerate(order):
            part = out[:, place * width : (place + 1) * width]
            for refs, low in ((near_out, 0), (far_out, half)):
                ref = refs[i] if len(refs) == 2 else refs[0].at[i]
                ref[...] = part[low : low + half].astype(ref.dtype)

    @pl.when(first)
    def _():
        run((0, 1))

    @pl.when(jnp.logical_not(first))
    def _():
        run((1, 0))


def pack_kernel(*refs):
    w_in, w_out = refs[6:]
    units = refs[0].shape[1]
    for i, ref in enumerate((refs[0], refs[3], refs[1], refs[4])):
        w_in[:, i * units : (i + 1) * units] = ref[...]
    w_out[:units] = refs[2][...]
    w_out[units:] = refs[5][...]


def pack(own, theirs):
    depth, units = own[0].shape
    return pl.pallas_call(
        pack_kernel,
        out_shape=[
            jax.ShapeDtypeStruct((depth, 4 * units), own[0].dtype),
            jax.ShapeDtypeStruct((2 * units, depth), own[0].dtype),
        ],
        in_specs=[VMEM] * 6,
        out_specs=[VMEM] * 2,
        compiler_params=pltpu.CompilerParams(vmem_limit_bytes=24 * 1024 * 1024),
    )(*own, *theirs)


def split_kernel(both_ref, a_ref, b_ref):
    a_ref[...] = both_ref[0]
    b_ref[...] = both_ref[1]


def split(both):
    part = jax.ShapeDtypeStruct(both.shape[1:], both.dtype)
    return pl.pallas_call(
        split_kernel, out_shape=[part] * 2, in_specs=[VMEM], out_specs=[VMEM] * 2
    )(both)


def expert_block(near, far, weights, near_types, far_types):
    half, width = near[0].shape[-2:]
    shapes = []
    for types in (near_types, far_types):
        part = (half, width) if len(types) == 2 else (2, half, width)
        shapes += [jax.ShapeDtypeStruct(part, t) for t in types]
    count = (len(near), len(far), len(near_types), len(far_types))
    return pl.pallas_call(
        functools.partial(expert_kernel, count),
        out_shape=shapes,
        in_specs=[VMEM] * (len(near) + len(far) + 2),
        out_specs=[VMEM] * len(shapes),
        compiler_params=pltpu.CompilerParams(vmem_limit_bytes=8 * 1024 * 1024),
    )(*near, *far, *weights)


def dense_body(tokens, expert_ids, gate_fixed, w_gate, w_up, w_down):
    tie = lax.optimization_barrier
    f32, bf16 = jnp.float32, jnp.bfloat16
    core = lax.axis_index("tp")
    first = core == 0
    half = tokens.shape[0] // 2
    top, bottom = tokens[:half], tokens[half:]
    ids = jnp.where(first, expert_ids[:half], expert_ids[half:])
    scale = jnp.where(first, gate_fixed[:half], gate_fixed[half:]).astype(f32) / 2048.0
    offset = lax.axis_index("ep") - ids * ESPLIT
    here = jnp.where((offset >= 0) & (offset < ESPLIT), 1.0, 0.0)
    a0, b0, here, scale = tie(
        (jnp.where(first, top, bottom), jnp.where(first, bottom, top), here, scale)
    )
    here = here > 0
    b0 = swap_core(b0)
    b0, own = tie((b0, (w_gate[0], w_up[0], w_down[0])))
    theirs = tuple(swap_core(w) for w in own)

    def expert(near, far, near_types, far_types):
        return expert_block(near, far, weights, near_types, far_types)

    both0 = jnp.stack([a0, b0])
    z2 = swap(both0, 4)
    z1 = swap(both0, 2)
    held, theirs = tie((both0, theirs))
    x0 = swap(held, 1)
    weights = pack(own, theirs)
    z2, z1, x0, weights = tie((z2, z1, x0, weights))
    m6 = swap(z2, 2)
    m5 = swap(z2, 1)
    m6, m5, held = tie((m6, m5, x0))
    m7 = swap(m6, 1)
    m3 = swap(held, 2)
    p0, p1 = expert((both0,), (x0,), (f32,), (f32,))
    p4, p5 = expert((z2,), (m5,), (f32,), (bf16,))
    m7, m3, p0, p1, p4, p5 = tie((m7, m3, p0, p1, p4, p5))
    p6, p7 = expert((m6,), (m7,), (f32,), (bf16,))
    p7, p5, m3 = tie((p7, p5, m3))
    p2, p3 = expert((z1,), (m3,), (bf16,), (bf16,))
    r7 = swap(p7, 1).astype(f32)
    r5 = swap(p5, 1).astype(f32)
    r3 = swap(p3, 2).astype(f32)
    r6 = swap((p6 + r7).astype(bf16), 2).astype(f32)
    sent = (p4 + r6 + r5).astype(bf16)
    sent, p2, p1, r3 = tie((sent, p2, p1, r3))
    other = swap(sent, 4).astype(f32)
    r2 = swap(p2, 2).astype(f32)
    r1 = swap((p1 + r3).astype(bf16), 1).astype(f32)
    near = p0 + r2 + r1
    near_a, near_b = near[0], near[1]
    other_a, other_b = other[0], other[1]
    left = (jnp.where(here, near_a, other_a) * scale).astype(bf16)
    right = (jnp.where(here, near_b, other_b) * scale).astype(bf16)
    got = swap_core(right)
    return jnp.concatenate([jnp.where(first, left, got), jnp.where(first, got, left)], axis=0)


def routed_body(tokens, expert_ids, gate_fixed, w_gate, w_up, w_down):
    ep_count = lax.axis_size("ep")
    tok_dev, topk = expert_ids.shape
    experts = ep_count // ESPLIT
    capacity = max(2, min(tok_dev, 2 * tok_dev * topk // experts))
    flat_ids = expert_ids.reshape(-1)
    slot_index = flat_ids * capacity + earlier_ranks(flat_ids)
    chooser = (slot_index[None, :] == jnp.arange(experts * capacity)[:, None]).astype(jnp.bfloat16)
    whole = lax.all_gather(tokens, "tp", axis=1, tiled=True)
    width = whole.shape[1]
    routed_rows = jnp.repeat(whole, topk, axis=0)
    grouped = jnp.dot(chooser, routed_rows, preferred_element_type=jnp.float32).astype(jnp.bfloat16)
    grouped = grouped.reshape(experts, 1, capacity, width)
    copies = jnp.broadcast_to(grouped, (experts, ESPLIT, capacity, width))
    arrived = lax.all_to_all(
        copies.reshape(ep_count, capacity, width), "ep", split_axis=0, concat_axis=0, tiled=True
    )
    expert_rows = arrived.reshape(ep_count * capacity, arrived.shape[2])
    gate_act = jnp.dot(expert_rows, w_gate[0], preferred_element_type=jnp.float32)
    up_act = jnp.dot(expert_rows, w_up[0], preferred_element_type=jnp.float32)
    hidden = (jax.nn.silu(gate_act) * up_act).astype(jnp.bfloat16)
    partial_out = jnp.dot(hidden, w_down[0], preferred_element_type=jnp.float32).astype(
        jnp.bfloat16
    )
    summed = (
        lax.psum_scatter(partial_out, "tp", scatter_dimension=1, tiled=True)
        .astype(jnp.float32)
        .astype(jnp.bfloat16)
    )
    returned = lax.all_to_all(
        summed.reshape(ep_count, capacity, summed.shape[1]),
        "ep",
        split_axis=0,
        concat_axis=0,
        tiled=True,
    )
    quarters = jnp.sum(
        returned.reshape(experts, ESPLIT, capacity, returned.shape[2]).astype(jnp.float32), axis=1
    )
    quarters = quarters.reshape(experts * capacity, returned.shape[2])
    weights_route = gate_fixed.reshape(-1).astype(jnp.float32) / 2048.0
    routed = quarters[slot_index] * weights_route[:, None]
    return jnp.sum(routed.reshape(tok_dev, topk, routed.shape[1]), axis=1).astype(jnp.bfloat16)


def body(tokens, expert_ids, *rest):
    experts = lax.axis_size("ep") // ESPLIT
    dense = experts == 2 and expert_ids.shape[1] == 1
    return (dense_body if dense else routed_body)(tokens, expert_ids, *rest)


def solution(mesh):
    placed = (
        P(("groups", "ep"), "tp"),
        P(("groups", "ep"), None),
        P(("groups", "ep"), None),
        P("ep", None, "tp"),
        P("ep", None, "tp"),
        P("ep", "tp", None),
    )
    return jax.shard_map(
        body, mesh=mesh, in_specs=placed, out_specs=P(("groups", "ep"), "tp"), check_vma=False
    )
```

```python
import functools

import jax
import jax.numpy as jnp
from jax import lax
from jax.experimental import pallas as pl
from jax.experimental.pallas import tpu as pltpu
from jax.sharding import PartitionSpec as P

ESPLIT = 4
FLOPS_US = 1.15e9
VMEM = pl.BlockSpec(memory_space=pltpu.VMEM)


def earlier_ranks(labels):
    position = jnp.arange(labels.shape[0])
    matches = (labels[:, None] == labels[None, :]) & (position[:, None] < position[None, :])
    return jnp.sum(matches, axis=0)


def swap(value, bit):
    pairs = [(i, i ^ bit) for i in range(lax.axis_size("ep"))]
    return lax.ppermute(value, "ep", pairs)


def swap_of(value, bit, core):
    pairs = [(2 * i + core, 2 * (i ^ bit) + core) for i in range(lax.axis_size("ep"))]
    return lax.ppermute(value, ("ep", "tp"), pairs)


def swap_core(value):
    return lax.ppermute(value, "tp", [(0, 1), (1, 0)])


def pack_kernel(turn, *refs):
    w_in, w_out, sems = refs[-3:]
    units = refs[0].shape[1]
    gate, up = (w_in.at[:, i * units : (i + 1) * units] for i in (turn, 2 + turn))
    down = w_out.at[turn * units : (turn + 1) * units]
    copies = [
        pltpu.make_async_copy(ref, place, sems.at[i])
        for i, (ref, place) in enumerate(zip(refs[:3], (gate, up, down)))
    ]
    for copy in copies:
        copy.start()
    for copy in copies:
        copy.wait()


def pack(turn, parts, held=()):
    depth, units = parts[0].shape
    return pl.pallas_call(
        functools.partial(pack_kernel, turn),
        out_shape=[
            jax.ShapeDtypeStruct((depth, 4 * units), parts[0].dtype),
            jax.ShapeDtypeStruct((2 * units, depth), parts[0].dtype),
        ],
        in_specs=[pl.BlockSpec(memory_space=pl.ANY)] * 3 + [VMEM] * len(held),
        out_specs=[VMEM] * 2,
        scratch_shapes=[pltpu.SemaphoreType.DMA((3,))],
        input_output_aliases={3 + i: i for i in range(len(held))},
        compiler_params=pltpu.CompilerParams(vmem_limit_bytes=24 * 1024 * 1024),
    )(*parts, *held)


def expert_kernel(blocks_in, blocks_out, *refs):
    def take(shape):
        nonlocal refs
        taken, refs = refs[: len(shape)], refs[len(shape) :]
        return taken

    def parts(held):
        return held if len(held) == 2 else (held[0].at[0], held[0].at[1])

    blocks = [parts(take(block)) for block in blocks_in]
    w_in, w_out = take((None, None))
    sums = [parts(take(block)) for block in blocks_out]
    rows, width = blocks[0][0].shape
    first = lax.axis_index("tp") == 0

    def run(order):
        whole = jnp.concatenate(
            [jnp.concatenate([block[i][...] for block in blocks], axis=0) for i in order], axis=1
        )
        act = jnp.dot(whole, w_in[...], preferred_element_type=jnp.float32)
        units = act.shape[1] // 2
        gate, up = act[:, :units], act[:, units:]
        hidden = (gate / (1 + jnp.exp(-gate)) * up).astype(jnp.bfloat16)
        out = jnp.dot(hidden, w_out[...], preferred_element_type=jnp.float32)
        for place, i in enumerate(order):
            for j, held in enumerate(sums):
                part = out[j * rows : (j + 1) * rows, place * width : (place + 1) * width]
                held[i][...] = part.astype(held[i].dtype)

    @pl.when(first)
    def _():
        run((0, 1))

    @pl.when(jnp.logical_not(first))
    def _():
        run((1, 0))


def expert_block(blocks, weights, types, work):
    half, width = blocks[0][0].shape[-2:]
    shapes = [
        jax.ShapeDtypeStruct((half, width) if len(pair) == 2 else (2, half, width), t)
        for pair in types
        for t in pair
    ]
    flat = [array for block in blocks for array in block]
    return pl.pallas_call(
        functools.partial(
            expert_kernel, [(None,) * len(b) for b in blocks], [(None,) * len(t) for t in types]
        ),
        out_shape=shapes,
        in_specs=[VMEM] * (len(flat) + 2),
        out_specs=[VMEM] * len(shapes),
        cost_estimate=pl.CostEstimate(
            flops=int(work * FLOPS_US), bytes_accessed=0, transcendentals=0
        ),
        compiler_params=pltpu.CompilerParams(vmem_limit_bytes=16 * 1024 * 1024),
    )(*flat, *weights)


def part_kernel(index, both_ref, part_ref):
    part_ref[...] = both_ref[index]


def part_of(both, index):
    return pl.pallas_call(
        functools.partial(part_kernel, index),
        out_shape=jax.ShapeDtypeStruct(both.shape[1:], both.dtype),
        in_specs=[VMEM],
        out_specs=VMEM,
        cost_estimate=pl.CostEstimate(flops=int(FLOPS_US / 5), bytes_accessed=0, transcendentals=0),
        compiler_params=pltpu.CompilerParams(vmem_limit_bytes=4 * 1024 * 1024),
    )(both)


def widen_kernel(sum_ref, out_ref):
    out_ref[...] = sum_ref[...].astype(jnp.float32)


def widen(sums, work):
    return pl.pallas_call(
        widen_kernel,
        out_shape=jax.ShapeDtypeStruct(sums.shape, jnp.float32),
        in_specs=[VMEM],
        out_specs=VMEM,
        cost_estimate=pl.CostEstimate(
            flops=int(work * FLOPS_US), bytes_accessed=0, transcendentals=0
        ),
        compiler_params=pltpu.CompilerParams(vmem_limit_bytes=4 * 1024 * 1024),
    )(sums)


def add_kernel(one_ref, two_ref, out_ref):
    out_ref[...] = (one_ref[...] + two_ref[...].astype(jnp.float32)).astype(out_ref.dtype)


def add(one, two, work):
    return pl.pallas_call(
        add_kernel,
        out_shape=jax.ShapeDtypeStruct(two.shape, two.dtype),
        in_specs=[VMEM] * 2,
        out_specs=VMEM,
        cost_estimate=pl.CostEstimate(
            flops=int(work * FLOPS_US), bytes_accessed=0, transcendentals=0
        ),
        compiler_params=pltpu.CompilerParams(vmem_limit_bytes=4 * 1024 * 1024),
    )(one, two)


def pick_kernel(one_ref, two_ref, out_ref):
    first = lax.axis_index("tp") == 0

    @pl.when(first)
    def _():
        out_ref[...] = one_ref[...]

    @pl.when(jnp.logical_not(first))
    def _():
        out_ref[...] = two_ref[...]


def pick(one, two):
    return pl.pallas_call(
        pick_kernel,
        out_shape=jax.ShapeDtypeStruct(one.shape, one.dtype),
        in_specs=[VMEM] * 2,
        out_specs=VMEM,
        cost_estimate=pl.CostEstimate(flops=int(FLOPS_US / 5), bytes_accessed=0, transcendentals=0),
        compiler_params=pltpu.CompilerParams(vmem_limit_bytes=4 * 1024 * 1024),
    )(one, two)


def dense_body(tokens, expert_ids, gate_fixed, w_gate, w_up, w_down):
    tie = lax.optimization_barrier
    f32, bf16 = jnp.float32, jnp.bfloat16
    core = lax.axis_index("tp")
    first = core == 0
    half = tokens.shape[0] // 2
    top, bottom = tokens[:half], tokens[half:]
    a0, b0, place = tie(
        (jnp.where(first, top, bottom), jnp.where(first, bottom, top), lax.axis_index("ep"))
    )
    b0 = swap_core(b0)
    b0, own = tie((b0, (w_gate[0], w_up[0], w_down[0])))
    theirs = tuple(swap_core(w) for w in own)

    def expert(blocks, types, work=1.0):
        return expert_block(blocks, weights, types, work)

    both0 = jnp.stack([a0, b0])
    one, two, three = theirs
    z2 = swap(both0, 4)
    z1 = swap(both0, 2)
    held, one = tie((both0, one))
    x0 = swap(held, 1)
    packed = pack(0, own)
    weights = pack(1, (one, two, three), packed)
    z2, z1, x0, weights = tie((z2, z1, x0, weights))
    m6 = swap(z2, 2)
    m5 = swap(z2, 1)
    h6, h5 = part_of(m6, 0), part_of(m5, 1)
    z1, h5 = tie((z1, h5))
    m7a = swap(h6, 1)
    m7b = swap(h5, 2)
    m3 = swap(z1, 1)
    p4, p5 = expert(((z2,), (m5,)), ((f32,), (f32,)))
    m7a, m7b, p4, p5 = tie((m7a, m7b, p4, p5))
    p6, p7a, p7b = expert(((m6,), (m7a, m7b)), ((f32,), (bf16, bf16)))
    p0, p1, p2, p3 = expert(
        ((both0,), (x0,), (z1,), (m3,)), ((f32,), (bf16,), (f32,), (bf16,)), 1.0
    )
    r7a = swap(p7a, 1).astype(f32)
    r7b = swap(p7b, 2).astype(f32)
    s6 = jnp.stack([p6[0] + r7a, p6[1]]).astype(bf16)
    s5 = jnp.stack([p5[0], p5[1] + r7b]).astype(bf16)
    r6 = swap(s6, 2).astype(f32)
    r5 = swap(s5, 1).astype(f32)
    sent = (p4 + r6 + r5).astype(bf16)
    r3 = swap(p3, 1)
    s2 = add(p2, r3, 0.1)
    sent, p1 = tie((sent, p1))
    other = widen(swap(sent, 4), 0.5)
    r2 = swap(s2, 2)
    r1 = swap(p1, 1)
    near = p0 + r1.astype(f32) + r2.astype(f32)
    ids = jnp.where(first, expert_ids[:half], expert_ids[half:])
    scale = jnp.where(first, gate_fixed[:half], gate_fixed[half:]).astype(f32) / 2048.0
    offset = place - ids * ESPLIT
    here = (offset >= 0) & (offset < ESPLIT)
    mixed = jnp.where(here, near, other) * scale
    left, right = mixed[0].astype(bf16), mixed[1].astype(bf16)
    got = swap_core(right)
    return jnp.concatenate([jnp.where(first, left, got), jnp.where(first, got, left)], axis=0)


def routed_body(tokens, expert_ids, gate_fixed, w_gate, w_up, w_down):
    ep_count = lax.axis_size("ep")
    tok_dev, topk = expert_ids.shape
    experts = ep_count // ESPLIT
    capacity = max(2, min(tok_dev, 2 * tok_dev * topk // experts))
    flat_ids = expert_ids.reshape(-1)
    slot_index = flat_ids * capacity + earlier_ranks(flat_ids)
    chooser = (slot_index[None, :] == jnp.arange(experts * capacity)[:, None]).astype(jnp.bfloat16)
    whole = lax.all_gather(tokens, "tp", axis=1, tiled=True)
    width = whole.shape[1]
    routed_rows = jnp.repeat(whole, topk, axis=0)
    grouped = jnp.dot(chooser, routed_rows, preferred_element_type=jnp.float32).astype(jnp.bfloat16)
    grouped = grouped.reshape(experts, 1, capacity, width)
    copies = jnp.broadcast_to(grouped, (experts, ESPLIT, capacity, width))
    arrived = lax.all_to_all(
        copies.reshape(ep_count, capacity, width), "ep", split_axis=0, concat_axis=0, tiled=True
    )
    expert_rows = arrived.reshape(ep_count * capacity, arrived.shape[2])
    gate_act = jnp.dot(expert_rows, w_gate[0], preferred_element_type=jnp.float32)
    up_act = jnp.dot(expert_rows, w_up[0], preferred_element_type=jnp.float32)
    hidden = (jax.nn.silu(gate_act) * up_act).astype(jnp.bfloat16)
    partial_out = jnp.dot(hidden, w_down[0], preferred_element_type=jnp.float32).astype(
        jnp.bfloat16
    )
    summed = (
        lax.psum_scatter(partial_out, "tp", scatter_dimension=1, tiled=True)
        .astype(jnp.float32)
        .astype(jnp.bfloat16)
    )
    returned = lax.all_to_all(
        summed.reshape(ep_count, capacity, summed.shape[1]),
        "ep",
        split_axis=0,
        concat_axis=0,
        tiled=True,
    )
    quarters = jnp.sum(
        returned.reshape(experts, ESPLIT, capacity, returned.shape[2]).astype(jnp.float32), axis=1
    )
    quarters = quarters.reshape(experts * capacity, returned.shape[2])
    weights_route = gate_fixed.reshape(-1).astype(jnp.float32) / 2048.0
    routed = quarters[slot_index] * weights_route[:, None]
    return jnp.sum(routed.reshape(tok_dev, topk, routed.shape[1]), axis=1).astype(jnp.bfloat16)


def body(tokens, expert_ids, *rest):
    experts = lax.axis_size("ep") // ESPLIT
    dense = experts == 2 and expert_ids.shape[1] == 1
    return (dense_body if dense else routed_body)(tokens, expert_ids, *rest)


def solution(mesh):
    placed = (
        P(("groups", "ep"), "tp"),
        P(("groups", "ep"), None),
        P(("groups", "ep"), None),
        P("ep", None, "tp"),
        P("ep", None, "tp"),
        P("ep", "tp", None),
    )
    return jax.shard_map(
        body, mesh=mesh, in_specs=placed, out_specs=P(("groups", "ep"), "tp"), check_vma=False
    )
```

```python
import functools

import jax
import jax.numpy as jnp
from jax import lax
from jax.experimental import pallas as pl
from jax.experimental.pallas import tpu as pltpu
from jax.sharding import PartitionSpec as P

ESPLIT = 4
FLOPS_US = 1.15e9
VMEM = pl.BlockSpec(memory_space=pltpu.VMEM)


def earlier_ranks(labels):
    position = jnp.arange(labels.shape[0])
    matches = (labels[:, None] == labels[None, :]) & (position[:, None] < position[None, :])
    return jnp.sum(matches, axis=0)


def swap(value, bit):
    pairs = [(i, i ^ bit) for i in range(lax.axis_size("ep"))]
    return lax.ppermute(value, "ep", pairs)


def swap_of(value, bit, core):
    pairs = [(2 * i + core, 2 * (i ^ bit) + core) for i in range(lax.axis_size("ep"))]
    return lax.ppermute(value, ("ep", "tp"), pairs)


def swap_core(value):
    return lax.ppermute(value, "tp", [(0, 1), (1, 0)])


def pack_kernel(gate_ref, up_ref, down_ref, pack_ref, sems):
    depth, units = gate_ref.shape
    pairs = [(gate_ref, pack_ref.at[:, :units]), (up_ref, pack_ref.at[:, units : 2 * units])]
    for at in range(0, depth, units):
        pairs.append((down_ref.at[:, at : at + units], pack_ref.at[at : at + units, 2 * units :]))
    copies = [pltpu.make_async_copy(*pair, sems.at[i]) for i, pair in enumerate(pairs)]
    for copy in copies:
        copy.start()
    for copy in copies:
        copy.wait()


def pack(gate, up, down):
    depth, units = gate.shape
    return pl.pallas_call(
        pack_kernel,
        out_shape=jax.ShapeDtypeStruct((depth, 3 * units), gate.dtype),
        in_specs=[pl.BlockSpec(memory_space=pl.ANY)] * 3,
        out_specs=VMEM,
        scratch_shapes=[pltpu.SemaphoreType.DMA((2 + depth // units,))],
        cost_estimate=pl.CostEstimate(flops=int(2 * FLOPS_US), bytes_accessed=0, transcendentals=0),
        compiler_params=pltpu.CompilerParams(vmem_limit_bytes=8 * 1024 * 1024),
    )(gate, up, down)


def expert_kernel(blocks_in, blocks_out, *refs):
    def take(shape):
        nonlocal refs
        taken, refs = refs[: len(shape)], refs[len(shape) :]
        return taken

    def parts(held):
        return held if len(held) == 2 else (held[0].at[0], held[0].at[1])

    blocks = [parts(take(block)) for block in blocks_in]
    packs = take((None, None))
    sums = [parts(take(block)) for block in blocks_out]
    rows, width = blocks[0][0].shape
    first = lax.axis_index("tp") == 0

    def run(order):
        whole = jnp.concatenate(
            [jnp.concatenate([block[i][...] for block in blocks], axis=0) for i in order], axis=1
        )
        out = None
        for held in packs:
            depth, units = held.shape[0], held.shape[1] // 3
            act = jnp.dot(whole, held[:, : 2 * units], preferred_element_type=jnp.float32)
            w_out = jnp.concatenate(
                [held[at : at + units, 2 * units :] for at in range(0, depth, units)], axis=1
            )
            gate, up = act[:, :units], act[:, units:]
            hidden = (gate / (1 + jnp.exp(-gate)) * up).astype(jnp.bfloat16)
            part = jnp.dot(hidden, w_out, preferred_element_type=jnp.float32)
            out = part if out is None else out + part
        for place, i in enumerate(order):
            for j, held in enumerate(sums):
                part = out[j * rows : (j + 1) * rows, place * width : (place + 1) * width]
                held[i][...] = part.astype(held[i].dtype)

    @pl.when(first)
    def _():
        run((0, 1))

    @pl.when(jnp.logical_not(first))
    def _():
        run((1, 0))


def expert_block(blocks, weights, types, work):
    half, width = blocks[0][0].shape[-2:]
    shapes = [
        jax.ShapeDtypeStruct((half, width) if len(pair) == 2 else (2, half, width), t)
        for pair in types
        for t in pair
    ]
    flat = [array for block in blocks for array in block]
    return pl.pallas_call(
        functools.partial(
            expert_kernel, [(None,) * len(b) for b in blocks], [(None,) * len(t) for t in types]
        ),
        out_shape=shapes,
        in_specs=[VMEM] * (len(flat) + 2),
        out_specs=[VMEM] * len(shapes),
        cost_estimate=pl.CostEstimate(
            flops=int(work * FLOPS_US), bytes_accessed=0, transcendentals=0
        ),
        compiler_params=pltpu.CompilerParams(vmem_limit_bytes=16 * 1024 * 1024),
    )(*flat, *weights)


def part_kernel(index, both_ref, part_ref):
    part_ref[...] = both_ref[index]


def part_of(both, index):
    return pl.pallas_call(
        functools.partial(part_kernel, index),
        out_shape=jax.ShapeDtypeStruct(both.shape[1:], both.dtype),
        in_specs=[VMEM],
        out_specs=VMEM,
        cost_estimate=pl.CostEstimate(flops=int(FLOPS_US / 5), bytes_accessed=0, transcendentals=0),
        compiler_params=pltpu.CompilerParams(vmem_limit_bytes=4 * 1024 * 1024),
    )(both)


def cast_kernel(from_ref, to_ref):
    to_ref[...] = from_ref[...].astype(to_ref.dtype)


def cast(array, dtype, work):
    return pl.pallas_call(
        cast_kernel,
        out_shape=jax.ShapeDtypeStruct(array.shape, dtype),
        in_specs=[VMEM],
        out_specs=VMEM,
        cost_estimate=pl.CostEstimate(
            flops=int(work * FLOPS_US), bytes_accessed=0, transcendentals=0
        ),
        compiler_params=pltpu.CompilerParams(vmem_limit_bytes=4 * 1024 * 1024),
    )(array)


def add_kernel(one_ref, two_ref, out_ref):
    out_ref[...] = (one_ref[...] + two_ref[...].astype(jnp.float32)).astype(out_ref.dtype)


def add(one, two, work):
    return pl.pallas_call(
        add_kernel,
        out_shape=jax.ShapeDtypeStruct(two.shape, two.dtype),
        in_specs=[VMEM] * 2,
        out_specs=VMEM,
        cost_estimate=pl.CostEstimate(
            flops=int(work * FLOPS_US), bytes_accessed=0, transcendentals=0
        ),
        compiler_params=pltpu.CompilerParams(vmem_limit_bytes=4 * 1024 * 1024),
    )(one, two)


def pick_kernel(one_ref, two_ref, out_ref):
    first = lax.axis_index("tp") == 0

    @pl.when(first)
    def _():
        out_ref[...] = one_ref[...]

    @pl.when(jnp.logical_not(first))
    def _():
        out_ref[...] = two_ref[...]


def pick(one, two):
    return pl.pallas_call(
        pick_kernel,
        out_shape=jax.ShapeDtypeStruct(one.shape, one.dtype),
        in_specs=[VMEM] * 2,
        out_specs=VMEM,
        cost_estimate=pl.CostEstimate(flops=int(FLOPS_US / 5), bytes_accessed=0, transcendentals=0),
        compiler_params=pltpu.CompilerParams(vmem_limit_bytes=4 * 1024 * 1024),
    )(one, two)


def dense_body(tokens, expert_ids, gate_fixed, w_gate, w_up, w_down):
    tie = lax.optimization_barrier
    f32, bf16 = jnp.float32, jnp.bfloat16
    core = lax.axis_index("tp")
    first = core == 0
    half = tokens.shape[0] // 2
    top, bottom = tokens[:half], tokens[half:]
    a0, b0, place = tie(
        (jnp.where(first, top, bottom), jnp.where(first, bottom, top), lax.axis_index("ep"))
    )
    b0 = swap_core(b0)
    ours = pack(w_gate[0], w_up[0], w_down[0])

    def expert(blocks, types, work=1.0):
        return expert_block(blocks, weights, types, work)

    both0 = jnp.stack([a0, b0])
    z2 = swap(both0, 4)
    z1 = swap(both0, 2)
    x0 = swap(both0, 1)
    z2, z1, x0, ours = tie((z2, z1, x0, ours))
    weights = [ours, swap_core(ours)]
    m6 = swap(z2, 2)
    m5 = swap(z2, 1)
    m6a, m5b = part_of(m6, 0), part_of(m5, 1)
    m5b, held = tie((m5b, x0))
    m3 = swap(held, 2)
    m7a = swap(m6a, 1)
    m7b = swap(m5b, 2)
    p4, p5 = expert(((z2,), (m5,)), ((f32,), (f32,)))
    m7a, m7b, p4, p5 = tie((m7a, m7b, p4, p5))
    p6, p7a, p7b = expert(((m6,), (m7a, m7b)), ((f32,), (bf16, bf16)))
    p0, p1, p2, p3 = expert(
        ((both0,), (x0,), (z1,), (m3,)), ((f32,), (bf16,), (f32,), (bf16,)), 1.0
    )
    r7a = swap(p7a, 1)
    r7b = swap(p7b, 2)
    r7a, p1, p2, p3 = tie((r7a, p1, p2, p3))
    s6 = jnp.stack([p6[0] + r7a.astype(f32), p6[1]]).astype(bf16)
    s5 = jnp.stack([p5[0], p5[1] + r7b.astype(f32)]).astype(bf16)
    r6 = swap(s6, 2).astype(f32)
    r5 = swap(s5, 1).astype(f32)
    sent = (p4 + r6 + r5).astype(bf16)
    r3 = swap(p3, 1)
    s2 = add(p2, r3, 0.1)
    sent, p1 = tie((sent, p1))
    other = cast(swap(sent, 4), f32, 0.5)
    r2 = swap(s2, 2)
    r1 = swap(p1, 1)
    near = p0 + r1.astype(f32) + r2.astype(f32)
    ids = jnp.where(first, expert_ids[:half], expert_ids[half:])
    scale = jnp.where(first, gate_fixed[:half], gate_fixed[half:]).astype(f32) / 2048.0
    offset = place - ids * ESPLIT
    here = (offset >= 0) & (offset < ESPLIT)
    mixed = jnp.where(here, near, other) * scale
    left, right = mixed[0].astype(bf16), mixed[1].astype(bf16)
    got = swap_core(right)
    return jnp.concatenate([jnp.where(first, left, got), jnp.where(first, got, left)], axis=0)


def routed_body(tokens, expert_ids, gate_fixed, w_gate, w_up, w_down):
    ep_count = lax.axis_size("ep")
    tok_dev, topk = expert_ids.shape
    experts = ep_count // ESPLIT
    capacity = max(2, min(tok_dev, 2 * tok_dev * topk // experts))
    flat_ids = expert_ids.reshape(-1)
    slot_index = flat_ids * capacity + earlier_ranks(flat_ids)
    chooser = (slot_index[None, :] == jnp.arange(experts * capacity)[:, None]).astype(jnp.bfloat16)
    whole = lax.all_gather(tokens, "tp", axis=1, tiled=True)
    width = whole.shape[1]
    routed_rows = jnp.repeat(whole, topk, axis=0)
    grouped = jnp.dot(chooser, routed_rows, preferred_element_type=jnp.float32).astype(jnp.bfloat16)
    grouped = grouped.reshape(experts, 1, capacity, width)
    copies = jnp.broadcast_to(grouped, (experts, ESPLIT, capacity, width))
    arrived = lax.all_to_all(
        copies.reshape(ep_count, capacity, width), "ep", split_axis=0, concat_axis=0, tiled=True
    )
    expert_rows = arrived.reshape(ep_count * capacity, arrived.shape[2])
    gate_act = jnp.dot(expert_rows, w_gate[0], preferred_element_type=jnp.float32)
    up_act = jnp.dot(expert_rows, w_up[0], preferred_element_type=jnp.float32)
    hidden = (jax.nn.silu(gate_act) * up_act).astype(jnp.bfloat16)
    partial_out = jnp.dot(hidden, w_down[0], preferred_element_type=jnp.float32).astype(
        jnp.bfloat16
    )
    summed = (
        lax.psum_scatter(partial_out, "tp", scatter_dimension=1, tiled=True)
        .astype(jnp.float32)
        .astype(jnp.bfloat16)
    )
    returned = lax.all_to_all(
        summed.reshape(ep_count, capacity, summed.shape[1]),
        "ep",
        split_axis=0,
        concat_axis=0,
        tiled=True,
    )
    quarters = jnp.sum(
        returned.reshape(experts, ESPLIT, capacity, returned.shape[2]).astype(jnp.float32), axis=1
    )
    quarters = quarters.reshape(experts * capacity, returned.shape[2])
    weights_route = gate_fixed.reshape(-1).astype(jnp.float32) / 2048.0
    routed = quarters[slot_index] * weights_route[:, None]
    return jnp.sum(routed.reshape(tok_dev, topk, routed.shape[1]), axis=1).astype(jnp.bfloat16)


def body(tokens, expert_ids, *rest):
    experts = lax.axis_size("ep") // ESPLIT
    dense = experts == 2 and expert_ids.shape[1] == 1
    return (dense_body if dense else routed_body)(tokens, expert_ids, *rest)


def solution(mesh):
    placed = (
        P(("groups", "ep"), "tp"),
        P(("groups", "ep"), None),
        P(("groups", "ep"), None),
        P("ep", None, "tp"),
        P("ep", None, "tp"),
        P("ep", "tp", None),
    )
    return jax.shard_map(
        body, mesh=mesh, in_specs=placed, out_specs=P(("groups", "ep"), "tp"), check_vma=False
    )
```

```python
import functools

import jax
import jax.numpy as jnp
from jax import lax
from jax.experimental import pallas as pl
from jax.experimental.pallas import tpu as pltpu
from jax.sharding import PartitionSpec as P

ESPLIT = 4
FLOPS_US = 1.15e9
VMEM = pl.BlockSpec(memory_space=pltpu.VMEM)


def earlier_ranks(labels):
    position = jnp.arange(labels.shape[0])
    matches = (labels[:, None] == labels[None, :]) & (position[:, None] < position[None, :])
    return jnp.sum(matches, axis=0)


def swap(value, bit):
    pairs = [(i, i ^ bit) for i in range(lax.axis_size("ep"))]
    return lax.ppermute(value, "ep", pairs)


def swap_of(value, bit, core):
    pairs = [(2 * i + core, 2 * (i ^ bit) + core) for i in range(lax.axis_size("ep"))]
    return lax.ppermute(value, ("ep", "tp"), pairs)


def swap_core(value):
    return lax.ppermute(value, "tp", [(0, 1), (1, 0)])


def pack_kernel(gate_ref, up_ref, down_ref, pack_ref, sems):
    depth, units = gate_ref.shape
    pairs = [(gate_ref, pack_ref.at[:, :units]), (up_ref, pack_ref.at[:, units : 2 * units])]
    for at in range(0, depth, units):
        pairs.append((down_ref.at[:, at : at + units], pack_ref.at[at : at + units, 2 * units :]))
    copies = [pltpu.make_async_copy(*pair, sems.at[i]) for i, pair in enumerate(pairs)]
    for copy in copies:
        copy.start()
    for copy in copies:
        copy.wait()


def pack(gate, up, down):
    depth, units = gate.shape
    return pl.pallas_call(
        pack_kernel,
        out_shape=jax.ShapeDtypeStruct((depth, 3 * units), gate.dtype),
        in_specs=[pl.BlockSpec(memory_space=pl.ANY)] * 3,
        out_specs=VMEM,
        scratch_shapes=[pltpu.SemaphoreType.DMA((2 + depth // units,))],
        cost_estimate=pl.CostEstimate(flops=int(2 * FLOPS_US), bytes_accessed=0, transcendentals=0),
        compiler_params=pltpu.CompilerParams(vmem_limit_bytes=8 * 1024 * 1024),
    )(gate, up, down)


def expert_kernel(blocks_in, blocks_out, *refs):
    def take(shape):
        nonlocal refs
        taken, refs = refs[: len(shape)], refs[len(shape) :]
        return taken

    def parts(held):
        return held if len(held) == 2 else (held[0].at[0], held[0].at[1])

    blocks = [parts(take(block)) for block in blocks_in]
    packs = take((None, None))
    sums = [parts(take(block)) for block in blocks_out]
    rows, width = blocks[0][0].shape
    first = lax.axis_index("tp") == 0

    def run(order):
        whole = jnp.concatenate(
            [jnp.concatenate([block[i][...] for block in blocks], axis=0) for i in order], axis=1
        )
        out = None
        for held in packs:
            depth, units = held.shape[0], held.shape[1] // 3
            act = jnp.dot(whole, held[:, : 2 * units], preferred_element_type=jnp.float32)
            w_out = jnp.concatenate(
                [held[at : at + units, 2 * units :] for at in range(0, depth, units)], axis=1
            )
            gate, up = act[:, :units], act[:, units:]
            hidden = (gate / (1 + jnp.exp(-gate)) * up).astype(jnp.bfloat16)
            part = jnp.dot(hidden, w_out, preferred_element_type=jnp.float32)
            out = part if out is None else out + part
        for place, i in enumerate(order):
            for j, held in enumerate(sums):
                part = out[j * rows : (j + 1) * rows, place * width : (place + 1) * width]
                held[i][...] = part.astype(held[i].dtype)

    @pl.when(first)
    def _():
        run((0, 1))

    @pl.when(jnp.logical_not(first))
    def _():
        run((1, 0))


def expert_block(blocks, weights, types, work):
    half, width = blocks[0][0].shape[-2:]
    shapes = [
        jax.ShapeDtypeStruct((half, width) if len(pair) == 2 else (2, half, width), t)
        for pair in types
        for t in pair
    ]
    flat = [array for block in blocks for array in block]
    return pl.pallas_call(
        functools.partial(
            expert_kernel, [(None,) * len(b) for b in blocks], [(None,) * len(t) for t in types]
        ),
        out_shape=shapes,
        in_specs=[VMEM] * (len(flat) + 2),
        out_specs=[VMEM] * len(shapes),
        cost_estimate=pl.CostEstimate(
            flops=int(work * FLOPS_US), bytes_accessed=0, transcendentals=0
        ),
        compiler_params=pltpu.CompilerParams(vmem_limit_bytes=16 * 1024 * 1024),
    )(*flat, *weights)


def part_kernel(index, both_ref, part_ref):
    part_ref[...] = both_ref[index]


def part_of(both, index):
    return pl.pallas_call(
        functools.partial(part_kernel, index),
        out_shape=jax.ShapeDtypeStruct(both.shape[1:], both.dtype),
        in_specs=[VMEM],
        out_specs=VMEM,
        cost_estimate=pl.CostEstimate(flops=int(FLOPS_US / 5), bytes_accessed=0, transcendentals=0),
        compiler_params=pltpu.CompilerParams(vmem_limit_bytes=4 * 1024 * 1024),
    )(both)


def cast_kernel(from_ref, to_ref):
    to_ref[...] = from_ref[...].astype(to_ref.dtype)


def cast(array, dtype, work):
    return pl.pallas_call(
        cast_kernel,
        out_shape=jax.ShapeDtypeStruct(array.shape, dtype),
        in_specs=[VMEM],
        out_specs=VMEM,
        cost_estimate=pl.CostEstimate(
            flops=int(work * FLOPS_US), bytes_accessed=0, transcendentals=0
        ),
        compiler_params=pltpu.CompilerParams(vmem_limit_bytes=4 * 1024 * 1024),
    )(array)


def add_kernel(one_ref, two_ref, out_ref):
    out_ref[...] = (one_ref[...] + two_ref[...].astype(jnp.float32)).astype(out_ref.dtype)


def add(one, two, work):
    return pl.pallas_call(
        add_kernel,
        out_shape=jax.ShapeDtypeStruct(two.shape, two.dtype),
        in_specs=[VMEM] * 2,
        out_specs=VMEM,
        cost_estimate=pl.CostEstimate(
            flops=int(work * FLOPS_US), bytes_accessed=0, transcendentals=0
        ),
        compiler_params=pltpu.CompilerParams(vmem_limit_bytes=4 * 1024 * 1024),
    )(one, two)


def pick_kernel(one_ref, two_ref, out_ref):
    first = lax.axis_index("tp") == 0

    @pl.when(first)
    def _():
        out_ref[...] = one_ref[...]

    @pl.when(jnp.logical_not(first))
    def _():
        out_ref[...] = two_ref[...]


def pick(one, two):
    return pl.pallas_call(
        pick_kernel,
        out_shape=jax.ShapeDtypeStruct(one.shape, one.dtype),
        in_specs=[VMEM] * 2,
        out_specs=VMEM,
        cost_estimate=pl.CostEstimate(flops=int(FLOPS_US / 5), bytes_accessed=0, transcendentals=0),
        compiler_params=pltpu.CompilerParams(vmem_limit_bytes=4 * 1024 * 1024),
    )(one, two)


def dense_body(tokens, expert_ids, gate_fixed, w_gate, w_up, w_down):
    tie = lax.optimization_barrier
    f32, bf16 = jnp.float32, jnp.bfloat16
    core = lax.axis_index("tp")
    first = core == 0
    half = tokens.shape[0] // 2
    top, bottom = tokens[:half], tokens[half:]
    a0, b0, place = tie(
        (jnp.where(first, top, bottom), jnp.where(first, bottom, top), lax.axis_index("ep"))
    )
    b0 = swap_core(b0)
    ours = pack(w_gate[0], w_up[0], w_down[0])

    def expert(blocks, types, work=1.0):
        return expert_block(blocks, weights, types, work)

    both0 = jnp.stack([a0, b0])
    z2a = cast(swap(a0, 4), bf16, 0.3)
    z2b = cast(swap(b0, 4), bf16, 0.3)
    z1 = swap(both0, 2)
    x0 = swap(both0, 1)
    z2a, z2b, z1, x0, ours = tie((z2a, z2b, z1, x0, ours))
    weights = [ours, swap_core(ours)]
    m5b = swap(z2b, 1)
    m5a = swap(z2a, 1)
    m6a = swap(z2a, 2)
    m6b = swap(z2b, 2)
    m5a, m6b = tie((m5a, m6b))
    m5b, held = tie((m5b, x0))
    m3 = swap(held, 2)
    m7a = swap(m6a, 1)
    m7b = swap(m5b, 2)
    p4, p5a, p5b = expert(((z2a, z2b), (m5a, m5b)), ((f32,), (bf16, f32)))
    m7a, m7b, p4, p5a, p5b = tie((m7a, m7b, p4, p5a, p5b))
    p6, p7a, p7b = expert(((m6a, m6b), (m7a, m7b)), ((f32,), (bf16, bf16)))
    p0, p1, p2, p3 = expert(
        ((both0,), (x0,), (z1,), (m3,)), ((f32,), (bf16,), (f32,), (bf16,)), 1.0
    )
    r7a = swap(p7a, 1)
    r7b = swap(p7b, 2)
    r7a, p1, p2, p3 = tie((r7a, p1, p2, p3))
    s6 = jnp.stack([p6[0] + r7a.astype(f32), p6[1]]).astype(bf16)
    r5a = swap(p5a, 1)
    r7b, r5a = tie((r7b, r5a))
    s5b = (p5b + r7b.astype(f32)).astype(bf16)
    r6 = swap(s6, 2).astype(f32)
    r5b = swap(s5b, 1)
    r5 = jnp.stack([r5a, r5b]).astype(f32)
    sent = (p4 + r6 + r5).astype(bf16)
    r3 = swap(p3, 1)
    s2 = add(p2, r3, 0.1)
    sent, p1 = tie((sent, p1))
    other = cast(swap(sent, 4), f32, 0.5)
    r2 = swap(s2, 2)
    r1 = swap(p1, 1)
    near = p0 + r1.astype(f32) + r2.astype(f32)
    ids = jnp.where(first, expert_ids[:half], expert_ids[half:])
    scale = jnp.where(first, gate_fixed[:half], gate_fixed[half:]).astype(f32) / 2048.0
    offset = place - ids * ESPLIT
    here = (offset >= 0) & (offset < ESPLIT)
    mixed = jnp.where(here, near, other) * scale
    left, right = mixed[0].astype(bf16), mixed[1].astype(bf16)
    got = swap_core(right)
    return jnp.concatenate([jnp.where(first, left, got), jnp.where(first, got, left)], axis=0)


def routed_body(tokens, expert_ids, gate_fixed, w_gate, w_up, w_down):
    ep_count = lax.axis_size("ep")
    tok_dev, topk = expert_ids.shape
    experts = ep_count // ESPLIT
    capacity = max(2, min(tok_dev, 2 * tok_dev * topk // experts))
    flat_ids = expert_ids.reshape(-1)
    slot_index = flat_ids * capacity + earlier_ranks(flat_ids)
    chooser = (slot_index[None, :] == jnp.arange(experts * capacity)[:, None]).astype(jnp.bfloat16)
    whole = lax.all_gather(tokens, "tp", axis=1, tiled=True)
    width = whole.shape[1]
    routed_rows = jnp.repeat(whole, topk, axis=0)
    grouped = jnp.dot(chooser, routed_rows, preferred_element_type=jnp.float32).astype(jnp.bfloat16)
    grouped = grouped.reshape(experts, 1, capacity, width)
    copies = jnp.broadcast_to(grouped, (experts, ESPLIT, capacity, width))
    arrived = lax.all_to_all(
        copies.reshape(ep_count, capacity, width), "ep", split_axis=0, concat_axis=0, tiled=True
    )
    expert_rows = arrived.reshape(ep_count * capacity, arrived.shape[2])
    gate_act = jnp.dot(expert_rows, w_gate[0], preferred_element_type=jnp.float32)
    up_act = jnp.dot(expert_rows, w_up[0], preferred_element_type=jnp.float32)
    hidden = (jax.nn.silu(gate_act) * up_act).astype(jnp.bfloat16)
    partial_out = jnp.dot(hidden, w_down[0], preferred_element_type=jnp.float32).astype(
        jnp.bfloat16
    )
    summed = (
        lax.psum_scatter(partial_out, "tp", scatter_dimension=1, tiled=True)
        .astype(jnp.float32)
        .astype(jnp.bfloat16)
    )
    returned = lax.all_to_all(
        summed.reshape(ep_count, capacity, summed.shape[1]),
        "ep",
        split_axis=0,
        concat_axis=0,
        tiled=True,
    )
    quarters = jnp.sum(
        returned.reshape(experts, ESPLIT, capacity, returned.shape[2]).astype(jnp.float32), axis=1
    )
    quarters = quarters.reshape(experts * capacity, returned.shape[2])
    weights_route = gate_fixed.reshape(-1).astype(jnp.float32) / 2048.0
    routed = quarters[slot_index] * weights_route[:, None]
    return jnp.sum(routed.reshape(tok_dev, topk, routed.shape[1]), axis=1).astype(jnp.bfloat16)


def body(tokens, expert_ids, *rest):
    experts = lax.axis_size("ep") // ESPLIT
    dense = experts == 2 and expert_ids.shape[1] == 1
    return (dense_body if dense else routed_body)(tokens, expert_ids, *rest)


def solution(mesh):
    placed = (
        P(("groups", "ep"), "tp"),
        P(("groups", "ep"), None),
        P(("groups", "ep"), None),
        P("ep", None, "tp"),
        P("ep", None, "tp"),
        P("ep", "tp", None),
    )
    return jax.shard_map(
        body, mesh=mesh, in_specs=placed, out_specs=P(("groups", "ep"), "tp"), check_vma=False
    )
```

```python
import functools

import jax
import jax.numpy as jnp
from jax import lax
from jax.experimental import pallas as pl
from jax.experimental.pallas import tpu as pltpu
from jax.sharding import PartitionSpec as P

ESPLIT = 4
FLOPS_US = 1.15e9
VMEM = pl.BlockSpec(memory_space=pltpu.VMEM)


def earlier_ranks(labels):
    position = jnp.arange(labels.shape[0])
    matches = (labels[:, None] == labels[None, :]) & (position[:, None] < position[None, :])
    return jnp.sum(matches, axis=0)


def swap(value, bit):
    pairs = [(i, i ^ bit) for i in range(lax.axis_size("ep"))]
    return lax.ppermute(value, "ep", pairs)


def swap_of(value, bit, core):
    pairs = [(2 * i + core, 2 * (i ^ bit) + core) for i in range(lax.axis_size("ep"))]
    return lax.ppermute(value, ("ep", "tp"), pairs)


def swap_core(value):
    return lax.ppermute(value, "tp", [(0, 1), (1, 0)])


def pack_kernel(gate_ref, up_ref, down_ref, pack_ref, sems):
    depth, units = gate_ref.shape
    pairs = [(gate_ref, pack_ref.at[:, :units]), (up_ref, pack_ref.at[:, units : 2 * units])]
    for at in range(0, depth, units):
        pairs.append((down_ref.at[:, at : at + units], pack_ref.at[at : at + units, 2 * units :]))
    copies = [pltpu.make_async_copy(*pair, sems.at[i]) for i, pair in enumerate(pairs)]
    for copy in copies:
        copy.start()
    for copy in copies:
        copy.wait()


def pack(gate, up, down):
    depth, units = gate.shape
    return pl.pallas_call(
        pack_kernel,
        out_shape=jax.ShapeDtypeStruct((depth, 3 * units), gate.dtype),
        in_specs=[pl.BlockSpec(memory_space=pl.ANY)] * 3,
        out_specs=VMEM,
        scratch_shapes=[pltpu.SemaphoreType.DMA((2 + depth // units,))],
        cost_estimate=pl.CostEstimate(flops=int(2 * FLOPS_US), bytes_accessed=0, transcendentals=0),
        compiler_params=pltpu.CompilerParams(vmem_limit_bytes=8 * 1024 * 1024),
    )(gate, up, down)


def expert_kernel(blocks_in, blocks_out, *refs):
    def take(shape):
        nonlocal refs
        taken, refs = refs[: len(shape)], refs[len(shape) :]
        return taken

    def parts(held):
        return held if len(held) == 2 else (held[0].at[0], held[0].at[1])

    blocks = [parts(take(block)) for block in blocks_in]
    packs = take((None, None))
    sums = [parts(take(block)) for block in blocks_out]
    rows, width = blocks[0][0].shape
    first = lax.axis_index("tp") == 0

    def run(order):
        whole = jnp.concatenate(
            [jnp.concatenate([block[i][...] for block in blocks], axis=0) for i in order], axis=1
        )
        out = None
        for held in packs:
            depth, units = held.shape[0], held.shape[1] // 3
            act = jnp.dot(whole, held[:, : 2 * units], preferred_element_type=jnp.float32)
            w_out = jnp.concatenate(
                [held[at : at + units, 2 * units :] for at in range(0, depth, units)], axis=1
            )
            gate, up = act[:, :units], act[:, units:]
            hidden = (gate / (1 + jnp.exp(-gate)) * up).astype(jnp.bfloat16)
            part = jnp.dot(hidden, w_out, preferred_element_type=jnp.float32)
            out = part if out is None else out + part
        for place, i in enumerate(order):
            for j, held in enumerate(sums):
                part = out[j * rows : (j + 1) * rows, place * width : (place + 1) * width]
                held[i][...] = part.astype(held[i].dtype)

    @pl.when(first)
    def _():
        run((0, 1))

    @pl.when(jnp.logical_not(first))
    def _():
        run((1, 0))


def expert_block(blocks, weights, types, work):
    half, width = blocks[0][0].shape[-2:]
    shapes = [
        jax.ShapeDtypeStruct((half, width) if len(pair) == 2 else (2, half, width), t)
        for pair in types
        for t in pair
    ]
    flat = [array for block in blocks for array in block]
    return pl.pallas_call(
        functools.partial(
            expert_kernel, [(None,) * len(b) for b in blocks], [(None,) * len(t) for t in types]
        ),
        out_shape=shapes,
        in_specs=[VMEM] * (len(flat) + 2),
        out_specs=[VMEM] * len(shapes),
        cost_estimate=pl.CostEstimate(
            flops=int(work * FLOPS_US), bytes_accessed=0, transcendentals=0
        ),
        compiler_params=pltpu.CompilerParams(vmem_limit_bytes=16 * 1024 * 1024),
    )(*flat, *weights)


def part_kernel(index, both_ref, part_ref):
    part_ref[...] = both_ref[index]


def part_of(both, index):
    return pl.pallas_call(
        functools.partial(part_kernel, index),
        out_shape=jax.ShapeDtypeStruct(both.shape[1:], both.dtype),
        in_specs=[VMEM],
        out_specs=VMEM,
        cost_estimate=pl.CostEstimate(flops=int(FLOPS_US / 5), bytes_accessed=0, transcendentals=0),
        compiler_params=pltpu.CompilerParams(vmem_limit_bytes=4 * 1024 * 1024),
    )(both)


def cast_kernel(from_ref, to_ref):
    to_ref[...] = from_ref[...].astype(to_ref.dtype)


def cast(array, dtype, work):
    return pl.pallas_call(
        cast_kernel,
        out_shape=jax.ShapeDtypeStruct(array.shape, dtype),
        in_specs=[VMEM],
        out_specs=VMEM,
        cost_estimate=pl.CostEstimate(
            flops=int(work * FLOPS_US), bytes_accessed=0, transcendentals=0
        ),
        compiler_params=pltpu.CompilerParams(vmem_limit_bytes=4 * 1024 * 1024),
    )(array)


def add_kernel(one_ref, two_ref, out_ref):
    out_ref[...] = (one_ref[...] + two_ref[...].astype(jnp.float32)).astype(out_ref.dtype)


def add(one, two, work):
    return pl.pallas_call(
        add_kernel,
        out_shape=jax.ShapeDtypeStruct(two.shape, two.dtype),
        in_specs=[VMEM] * 2,
        out_specs=VMEM,
        cost_estimate=pl.CostEstimate(
            flops=int(work * FLOPS_US), bytes_accessed=0, transcendentals=0
        ),
        compiler_params=pltpu.CompilerParams(vmem_limit_bytes=4 * 1024 * 1024),
    )(one, two)


def pick_kernel(one_ref, two_ref, out_ref):
    first = lax.axis_index("tp") == 0

    @pl.when(first)
    def _():
        out_ref[...] = one_ref[...]

    @pl.when(jnp.logical_not(first))
    def _():
        out_ref[...] = two_ref[...]


def pick(one, two):
    return pl.pallas_call(
        pick_kernel,
        out_shape=jax.ShapeDtypeStruct(one.shape, one.dtype),
        in_specs=[VMEM] * 2,
        out_specs=VMEM,
        cost_estimate=pl.CostEstimate(flops=int(FLOPS_US / 5), bytes_accessed=0, transcendentals=0),
        compiler_params=pltpu.CompilerParams(vmem_limit_bytes=4 * 1024 * 1024),
    )(one, two)


def dense_body(tokens, expert_ids, gate_fixed, w_gate, w_up, w_down):
    tie = lax.optimization_barrier
    f32, bf16 = jnp.float32, jnp.bfloat16
    core = lax.axis_index("tp")
    first = core == 0
    half = tokens.shape[0] // 2
    top, bottom = tokens[:half], tokens[half:]
    a0, b0, place = tie(
        (jnp.where(first, top, bottom), jnp.where(first, bottom, top), lax.axis_index("ep"))
    )
    b0 = swap_core(b0)
    ours = pack(w_gate[0], w_up[0], w_down[0])

    def expert(blocks, types, work=1.0):
        return expert_block(blocks, weights, types, work)

    both0 = jnp.stack([a0, b0])
    z2a = cast(swap(a0, 4), bf16, 0.3)
    z2b = cast(swap(b0, 4), bf16, 0.3)
    z1 = swap(both0, 2)
    x0 = swap(both0, 1)
    z2a, z2b, z1, x0, ours = tie((z2a, z2b, z1, x0, ours))
    weights = [ours, swap_core(ours)]
    m5b = swap(z2b, 1)
    m5a = swap(z2a, 1)
    m6a = swap(z2a, 2)
    m6b = swap(z2b, 2)
    m5a, m6b = tie((m5a, m6b))
    m5b, held = tie((m5b, x0))
    m3 = swap(held, 2)
    m7a = swap(m6a, 1)
    m7b = swap(m5b, 2)
    p4, p5a, p5b = expert(((z2a, z2b), (m5a, m5b)), ((f32,), (bf16, f32)))
    m7a, m7b, p4, p5a, p5b = tie((m7a, m7b, p4, p5a, p5b))
    p6, p7a, p7b = expert(((m6a, m6b), (m7a, m7b)), ((f32,), (bf16, bf16)))
    p0, p1, p2, p3 = expert(
        ((both0,), (x0,), (z1,), (m3,)), ((f32,), (bf16,), (f32,), (bf16,)), 1.0
    )
    r7a = swap(p7a, 1)
    r7b = swap(p7b, 2)
    r7a, p1, p2, p3 = tie((r7a, p1, p2, p3))
    s6 = jnp.stack([p6[0] + r7a.astype(f32), p6[1]]).astype(bf16)
    r5a = cast(swap(p5a, 1), bf16, 2.0)
    s5b = add(p5b, r7b, 1.0)
    r6 = swap(s6, 2).astype(f32)
    r5b = swap(s5b, 1)
    r5 = jnp.stack([r5a, r5b]).astype(f32)
    sent = (p4 + r6 + r5).astype(bf16)
    s5b, p3 = tie((s5b, p3))
    r3 = swap(p3, 1)
    s2 = add(p2, r3, 0.1)
    sent, p1 = tie((sent, p1))
    other = cast(swap(sent, 4), f32, 0.5)
    r2 = swap(s2, 2)
    r1 = swap(p1, 1)
    near = p0 + r1.astype(f32) + r2.astype(f32)
    ids = jnp.where(first, expert_ids[:half], expert_ids[half:])
    scale = jnp.where(first, gate_fixed[:half], gate_fixed[half:]).astype(f32) / 2048.0
    offset = place - ids * ESPLIT
    here = (offset >= 0) & (offset < ESPLIT)
    mixed = jnp.where(here, near, other) * scale
    left, right = mixed[0].astype(bf16), mixed[1].astype(bf16)
    got = swap_core(right)
    return jnp.concatenate([jnp.where(first, left, got), jnp.where(first, got, left)], axis=0)


def routed_body(tokens, expert_ids, gate_fixed, w_gate, w_up, w_down):
    ep_count = lax.axis_size("ep")
    tok_dev, topk = expert_ids.shape
    experts = ep_count // ESPLIT
    capacity = max(2, min(tok_dev, 2 * tok_dev * topk // experts))
    flat_ids = expert_ids.reshape(-1)
    slot_index = flat_ids * capacity + earlier_ranks(flat_ids)
    chooser = (slot_index[None, :] == jnp.arange(experts * capacity)[:, None]).astype(jnp.bfloat16)
    whole = lax.all_gather(tokens, "tp", axis=1, tiled=True)
    width = whole.shape[1]
    routed_rows = jnp.repeat(whole, topk, axis=0)
    grouped = jnp.dot(chooser, routed_rows, preferred_element_type=jnp.float32).astype(jnp.bfloat16)
    grouped = grouped.reshape(experts, 1, capacity, width)
    copies = jnp.broadcast_to(grouped, (experts, ESPLIT, capacity, width))
    arrived = lax.all_to_all(
        copies.reshape(ep_count, capacity, width), "ep", split_axis=0, concat_axis=0, tiled=True
    )
    expert_rows = arrived.reshape(ep_count * capacity, arrived.shape[2])
    gate_act = jnp.dot(expert_rows, w_gate[0], preferred_element_type=jnp.float32)
    up_act = jnp.dot(expert_rows, w_up[0], preferred_element_type=jnp.float32)
    hidden = (jax.nn.silu(gate_act) * up_act).astype(jnp.bfloat16)
    partial_out = jnp.dot(hidden, w_down[0], preferred_element_type=jnp.float32).astype(
        jnp.bfloat16
    )
    summed = (
        lax.psum_scatter(partial_out, "tp", scatter_dimension=1, tiled=True)
        .astype(jnp.float32)
        .astype(jnp.bfloat16)
    )
    returned = lax.all_to_all(
        summed.reshape(ep_count, capacity, summed.shape[1]),
        "ep",
        split_axis=0,
        concat_axis=0,
        tiled=True,
    )
    quarters = jnp.sum(
        returned.reshape(experts, ESPLIT, capacity, returned.shape[2]).astype(jnp.float32), axis=1
    )
    quarters = quarters.reshape(experts * capacity, returned.shape[2])
    weights_route = gate_fixed.reshape(-1).astype(jnp.float32) / 2048.0
    routed = quarters[slot_index] * weights_route[:, None]
    return jnp.sum(routed.reshape(tok_dev, topk, routed.shape[1]), axis=1).astype(jnp.bfloat16)


def body(tokens, expert_ids, *rest):
    experts = lax.axis_size("ep") // ESPLIT
    dense = experts == 2 and expert_ids.shape[1] == 1
    return (dense_body if dense else routed_body)(tokens, expert_ids, *rest)


def solution(mesh):
    placed = (
        P(("groups", "ep"), "tp"),
        P(("groups", "ep"), None),
        P(("groups", "ep"), None),
        P("ep", None, "tp"),
        P("ep", None, "tp"),
        P("ep", "tp", None),
    )
    return jax.shard_map(
        body, mesh=mesh, in_specs=placed, out_specs=P(("groups", "ep"), "tp"), check_vma=False
    )
```

```python
import functools

import jax
import jax.numpy as jnp
from jax import lax
from jax.experimental import pallas as pl
from jax.experimental.pallas import tpu as pltpu
from jax.sharding import PartitionSpec as P

ESPLIT = 4
FLOPS_US = 1.15e9
VMEM = pl.BlockSpec(memory_space=pltpu.VMEM)


def earlier_ranks(labels):
    position = jnp.arange(labels.shape[0])
    matches = (labels[:, None] == labels[None, :]) & (position[:, None] < position[None, :])
    return jnp.sum(matches, axis=0)


def swap(value, bit):
    pairs = [(i, i ^ bit) for i in range(lax.axis_size("ep"))]
    return lax.ppermute(value, "ep", pairs)


def swap_of(value, bit, core):
    pairs = [(2 * i + core, 2 * (i ^ bit) + core) for i in range(lax.axis_size("ep"))]
    return lax.ppermute(value, ("ep", "tp"), pairs)


def swap_core(value):
    return lax.ppermute(value, "tp", [(0, 1), (1, 0)])


def pack_kernel(gate_ref, up_ref, down_ref, pack_ref, sems):
    depth, units = gate_ref.shape
    pairs = [(gate_ref, pack_ref.at[:, :units]), (up_ref, pack_ref.at[:, units : 2 * units])]
    for at in range(0, depth, units):
        pairs.append((down_ref.at[:, at : at + units], pack_ref.at[at : at + units, 2 * units :]))
    copies = [pltpu.make_async_copy(*pair, sems.at[i]) for i, pair in enumerate(pairs)]
    for copy in copies:
        copy.start()
    for copy in copies:
        copy.wait()


def pack(gate, up, down):
    depth, units = gate.shape
    return pl.pallas_call(
        pack_kernel,
        out_shape=jax.ShapeDtypeStruct((depth, 3 * units), gate.dtype),
        in_specs=[pl.BlockSpec(memory_space=pl.ANY)] * 3,
        out_specs=VMEM,
        scratch_shapes=[pltpu.SemaphoreType.DMA((2 + depth // units,))],
        cost_estimate=pl.CostEstimate(flops=int(2 * FLOPS_US), bytes_accessed=0, transcendentals=0),
        compiler_params=pltpu.CompilerParams(vmem_limit_bytes=8 * 1024 * 1024),
    )(gate, up, down)


def expert_kernel(blocks_in, blocks_out, *refs):
    def take(shape):
        nonlocal refs
        taken, refs = refs[: len(shape)], refs[len(shape) :]
        return taken

    def parts(held):
        return held if len(held) == 2 else (held[0].at[0], held[0].at[1])

    blocks = [parts(take(block)) for block in blocks_in]
    packs = take((None, None))
    sums = [parts(take(block)) for block in blocks_out]
    rows, width = blocks[0][0].shape
    first = lax.axis_index("tp") == 0

    def run(order):
        whole = jnp.concatenate(
            [jnp.concatenate([block[i][...] for block in blocks], axis=0) for i in order], axis=1
        )
        out = None
        for held in packs:
            depth, units = held.shape[0], held.shape[1] // 3
            act = jnp.dot(whole, held[:, : 2 * units], preferred_element_type=jnp.float32)
            w_out = jnp.concatenate(
                [held[at : at + units, 2 * units :] for at in range(0, depth, units)], axis=1
            )
            gate, up = act[:, :units], act[:, units:]
            hidden = (gate / (1 + jnp.exp(-gate)) * up).astype(jnp.bfloat16)
            part = jnp.dot(hidden, w_out, preferred_element_type=jnp.float32)
            out = part if out is None else out + part
        for place, i in enumerate(order):
            for j, held in enumerate(sums):
                part = out[j * rows : (j + 1) * rows, place * width : (place + 1) * width]
                held[i][...] = part.astype(held[i].dtype)

    @pl.when(first)
    def _():
        run((0, 1))

    @pl.when(jnp.logical_not(first))
    def _():
        run((1, 0))


def expert_block(blocks, weights, types, work):
    half, width = blocks[0][0].shape[-2:]
    shapes = [
        jax.ShapeDtypeStruct((half, width) if len(pair) == 2 else (2, half, width), t)
        for pair in types
        for t in pair
    ]
    flat = [array for block in blocks for array in block]
    return pl.pallas_call(
        functools.partial(
            expert_kernel, [(None,) * len(b) for b in blocks], [(None,) * len(t) for t in types]
        ),
        out_shape=shapes,
        in_specs=[VMEM] * (len(flat) + 2),
        out_specs=[VMEM] * len(shapes),
        cost_estimate=pl.CostEstimate(
            flops=int(work * FLOPS_US), bytes_accessed=0, transcendentals=0
        ),
        compiler_params=pltpu.CompilerParams(vmem_limit_bytes=16 * 1024 * 1024),
    )(*flat, *weights)


def part_kernel(index, both_ref, part_ref):
    part_ref[...] = both_ref[index]


def part_of(both, index):
    return pl.pallas_call(
        functools.partial(part_kernel, index),
        out_shape=jax.ShapeDtypeStruct(both.shape[1:], both.dtype),
        in_specs=[VMEM],
        out_specs=VMEM,
        cost_estimate=pl.CostEstimate(flops=int(FLOPS_US / 5), bytes_accessed=0, transcendentals=0),
        compiler_params=pltpu.CompilerParams(vmem_limit_bytes=4 * 1024 * 1024),
    )(both)


def cast_kernel(from_ref, to_ref):
    to_ref[...] = from_ref[...].astype(to_ref.dtype)


def cast(array, dtype, work):
    return pl.pallas_call(
        cast_kernel,
        out_shape=jax.ShapeDtypeStruct(array.shape, dtype),
        in_specs=[VMEM],
        out_specs=VMEM,
        cost_estimate=pl.CostEstimate(
            flops=int(work * FLOPS_US), bytes_accessed=0, transcendentals=0
        ),
        compiler_params=pltpu.CompilerParams(vmem_limit_bytes=4 * 1024 * 1024),
    )(array)


def add_kernel(one_ref, two_ref, out_ref):
    out_ref[...] = (one_ref[...] + two_ref[...].astype(jnp.float32)).astype(out_ref.dtype)


def add(one, two, work):
    return pl.pallas_call(
        add_kernel,
        out_shape=jax.ShapeDtypeStruct(two.shape, two.dtype),
        in_specs=[VMEM] * 2,
        out_specs=VMEM,
        cost_estimate=pl.CostEstimate(
            flops=int(work * FLOPS_US), bytes_accessed=0, transcendentals=0
        ),
        compiler_params=pltpu.CompilerParams(vmem_limit_bytes=4 * 1024 * 1024),
    )(one, two)


def pick_kernel(one_ref, two_ref, out_ref):
    first = lax.axis_index("tp") == 0

    @pl.when(first)
    def _():
        out_ref[...] = one_ref[...]

    @pl.when(jnp.logical_not(first))
    def _():
        out_ref[...] = two_ref[...]


def pick(one, two):
    return pl.pallas_call(
        pick_kernel,
        out_shape=jax.ShapeDtypeStruct(one.shape, one.dtype),
        in_specs=[VMEM] * 2,
        out_specs=VMEM,
        cost_estimate=pl.CostEstimate(flops=int(FLOPS_US / 5), bytes_accessed=0, transcendentals=0),
        compiler_params=pltpu.CompilerParams(vmem_limit_bytes=4 * 1024 * 1024),
    )(one, two)


def dense_body(tokens, expert_ids, gate_fixed, w_gate, w_up, w_down):
    tie = lax.optimization_barrier
    f32, bf16 = jnp.float32, jnp.bfloat16
    core = lax.axis_index("tp")
    first = core == 0
    half = tokens.shape[0] // 2
    top, bottom = tokens[:half], tokens[half:]
    a0, b0, place = tie(
        (jnp.where(first, top, bottom), jnp.where(first, bottom, top), lax.axis_index("ep"))
    )
    b0 = swap_core(b0)
    ours = pack(w_gate[0], w_up[0], w_down[0])

    def expert(blocks, types, work=1.0):
        return expert_block(blocks, weights, types, work)

    both0 = jnp.stack([a0, b0])
    z2a = swap(a0, 4)
    z2b = cast(swap(b0, 4), bf16, 0.3)
    z1 = swap(both0, 2)
    x0 = swap(both0, 1)
    z2a, ours = tie((z2a, ours))
    m6a = cast(swap(z2a, 2), bf16, 40.0)
    m5a = swap(z2a, 1)
    z2b, z1, x0, ours = tie((z2b, z1, x0, ours))
    weights = [ours, swap_core(ours)]
    m5b = swap(z2b, 1)
    m6b = swap(z2b, 2)
    m5a, m6b = tie((m5a, m6b))
    m5b, held = tie((m5b, x0))
    m3 = swap(held, 2)
    m7a = swap(m6a, 1)
    m7b = swap(m5b, 2)
    p4, p5a, p5b = expert(((z2a, z2b), (m5a, m5b)), ((f32,), (bf16, f32)))
    m7a, m7b, p4, p5a, p5b = tie((m7a, m7b, p4, p5a, p5b))
    p6, p7a, p7b = expert(((m6a, m6b), (m7a, m7b)), ((f32,), (bf16, bf16)))
    p0, p1, p2, p3 = expert(
        ((both0,), (x0,), (z1,), (m3,)), ((f32,), (bf16,), (f32,), (bf16,)), 1.0
    )
    r7b = swap(p7b, 2)
    r7a = swap(p7a, 1)
    r7a, p1, p2, p3 = tie((r7a, p1, p2, p3))
    s6 = jnp.stack([p6[0] + r7a.astype(f32), p6[1]]).astype(bf16)
    r5a = cast(swap(p5a, 1), bf16, 2.0)
    s5b = add(p5b, r7b, 1.0)
    r6 = swap(s6, 2).astype(f32)
    r5b = swap(s5b, 1)
    r5 = jnp.stack([r5a, r5b]).astype(f32)
    sent = (p4 + r6 + r5).astype(bf16)
    s5b, p3 = tie((s5b, p3))
    r3 = swap(p3, 1)
    s2 = add(p2, r3, 0.1)
    sent, p1 = tie((sent, p1))
    other = cast(swap(sent, 4), f32, 0.5)
    r2 = swap(s2, 2)
    r1 = swap(p1, 1)
    near = p0 + r1.astype(f32) + r2.astype(f32)
    ids = jnp.where(first, expert_ids[:half], expert_ids[half:])
    scale = jnp.where(first, gate_fixed[:half], gate_fixed[half:]).astype(f32) / 2048.0
    offset = place - ids * ESPLIT
    here = (offset >= 0) & (offset < ESPLIT)
    mixed = jnp.where(here, near, other) * scale
    left, right = mixed[0].astype(bf16), mixed[1].astype(bf16)
    got = swap_core(right)
    return jnp.concatenate([jnp.where(first, left, got), jnp.where(first, got, left)], axis=0)


def routed_body(tokens, expert_ids, gate_fixed, w_gate, w_up, w_down):
    ep_count = lax.axis_size("ep")
    tok_dev, topk = expert_ids.shape
    experts = ep_count // ESPLIT
    capacity = max(2, min(tok_dev, 2 * tok_dev * topk // experts))
    flat_ids = expert_ids.reshape(-1)
    slot_index = flat_ids * capacity + earlier_ranks(flat_ids)
    chooser = (slot_index[None, :] == jnp.arange(experts * capacity)[:, None]).astype(jnp.bfloat16)
    whole = lax.all_gather(tokens, "tp", axis=1, tiled=True)
    width = whole.shape[1]
    routed_rows = jnp.repeat(whole, topk, axis=0)
    grouped = jnp.dot(chooser, routed_rows, preferred_element_type=jnp.float32).astype(jnp.bfloat16)
    grouped = grouped.reshape(experts, 1, capacity, width)
    copies = jnp.broadcast_to(grouped, (experts, ESPLIT, capacity, width))
    arrived = lax.all_to_all(
        copies.reshape(ep_count, capacity, width), "ep", split_axis=0, concat_axis=0, tiled=True
    )
    expert_rows = arrived.reshape(ep_count * capacity, arrived.shape[2])
    gate_act = jnp.dot(expert_rows, w_gate[0], preferred_element_type=jnp.float32)
    up_act = jnp.dot(expert_rows, w_up[0], preferred_element_type=jnp.float32)
    hidden = (jax.nn.silu(gate_act) * up_act).astype(jnp.bfloat16)
    partial_out = jnp.dot(hidden, w_down[0], preferred_element_type=jnp.float32).astype(
        jnp.bfloat16
    )
    summed = (
        lax.psum_scatter(partial_out, "tp", scatter_dimension=1, tiled=True)
        .astype(jnp.float32)
        .astype(jnp.bfloat16)
    )
    returned = lax.all_to_all(
        summed.reshape(ep_count, capacity, summed.shape[1]),
        "ep",
        split_axis=0,
        concat_axis=0,
        tiled=True,
    )
    quarters = jnp.sum(
        returned.reshape(experts, ESPLIT, capacity, returned.shape[2]).astype(jnp.float32), axis=1
    )
    quarters = quarters.reshape(experts * capacity, returned.shape[2])
    weights_route = gate_fixed.reshape(-1).astype(jnp.float32) / 2048.0
    routed = quarters[slot_index] * weights_route[:, None]
    return jnp.sum(routed.reshape(tok_dev, topk, routed.shape[1]), axis=1).astype(jnp.bfloat16)


def body(tokens, expert_ids, *rest):
    experts = lax.axis_size("ep") // ESPLIT
    dense = experts == 2 and expert_ids.shape[1] == 1
    return (dense_body if dense else routed_body)(tokens, expert_ids, *rest)


def solution(mesh):
    placed = (
        P(("groups", "ep"), "tp"),
        P(("groups", "ep"), None),
        P(("groups", "ep"), None),
        P("ep", None, "tp"),
        P("ep", None, "tp"),
        P("ep", "tp", None),
    )
    return jax.shard_map(
        body, mesh=mesh, in_specs=placed, out_specs=P(("groups", "ep"), "tp"), check_vma=False
    )
```

```python
import functools

import jax
import jax.numpy as jnp
from jax import lax
from jax.experimental import pallas as pl
from jax.experimental.pallas import tpu as pltpu
from jax.sharding import PartitionSpec as P

ESPLIT = 4
FLOPS_US = 1.15e9
VMEM = pl.BlockSpec(memory_space=pltpu.VMEM)


def earlier_ranks(labels):
    position = jnp.arange(labels.shape[0])
    matches = (labels[:, None] == labels[None, :]) & (position[:, None] < position[None, :])
    return jnp.sum(matches, axis=0)


def swap(value, bit):
    pairs = [(i, i ^ bit) for i in range(lax.axis_size("ep"))]
    return lax.ppermute(value, "ep", pairs)


def swap_of(value, bit, core):
    pairs = [(2 * i + core, 2 * (i ^ bit) + core) for i in range(lax.axis_size("ep"))]
    return lax.ppermute(value, ("ep", "tp"), pairs)


def swap_core(value):
    return lax.ppermute(value, "tp", [(0, 1), (1, 0)])


def pack_kernel(gate_ref, up_ref, down_ref, pack_ref, sems):
    depth, units = gate_ref.shape
    pairs = [(gate_ref, pack_ref.at[:, :units]), (up_ref, pack_ref.at[:, units : 2 * units])]
    for at in range(0, depth, units):
        pairs.append((down_ref.at[:, at : at + units], pack_ref.at[at : at + units, 2 * units :]))
    copies = [pltpu.make_async_copy(*pair, sems.at[i]) for i, pair in enumerate(pairs)]
    for copy in copies:
        copy.start()
    for copy in copies:
        copy.wait()


def pack(gate, up, down):
    depth, units = gate.shape
    return pl.pallas_call(
        pack_kernel,
        out_shape=jax.ShapeDtypeStruct((depth, 3 * units), gate.dtype),
        in_specs=[pl.BlockSpec(memory_space=pl.ANY)] * 3,
        out_specs=VMEM,
        scratch_shapes=[pltpu.SemaphoreType.DMA((2 + depth // units,))],
        cost_estimate=pl.CostEstimate(flops=int(2 * FLOPS_US), bytes_accessed=0, transcendentals=0),
        compiler_params=pltpu.CompilerParams(vmem_limit_bytes=8 * 1024 * 1024),
    )(gate, up, down)


def expert_kernel(blocks_in, blocks_out, *refs):
    def take(shape):
        nonlocal refs
        taken, refs = refs[: len(shape)], refs[len(shape) :]
        return taken

    def parts(held):
        return held if len(held) == 2 else (held[0].at[0], held[0].at[1])

    blocks = [parts(take(block)) for block in blocks_in]
    packs = take((None, None))
    sums = [parts(take(block)) for block in blocks_out]
    rows, width = blocks[0][0].shape
    first = lax.axis_index("tp") == 0

    def run(order):
        whole = jnp.concatenate(
            [jnp.concatenate([block[i][...] for block in blocks], axis=0) for i in order], axis=1
        )
        out = None
        for held in packs:
            depth, units = held.shape[0], held.shape[1] // 3
            act = jnp.dot(whole, held[:, : 2 * units], preferred_element_type=jnp.float32)
            w_out = jnp.concatenate(
                [held[at : at + units, 2 * units :] for at in range(0, depth, units)], axis=1
            )
            gate, up = act[:, :units], act[:, units:]
            hidden = (gate / (1 + jnp.exp(-gate)) * up).astype(jnp.bfloat16)
            part = jnp.dot(hidden, w_out, preferred_element_type=jnp.float32)
            out = part if out is None else out + part
        for place, i in enumerate(order):
            for j, held in enumerate(sums):
                part = out[j * rows : (j + 1) * rows, place * width : (place + 1) * width]
                held[i][...] = part.astype(held[i].dtype)

    @pl.when(first)
    def _():
        run((0, 1))

    @pl.when(jnp.logical_not(first))
    def _():
        run((1, 0))


def expert_block(blocks, weights, types, work):
    half, width = blocks[0][0].shape[-2:]
    shapes = [
        jax.ShapeDtypeStruct((half, width) if len(pair) == 2 else (2, half, width), t)
        for pair in types
        for t in pair
    ]
    flat = [array for block in blocks for array in block]
    return pl.pallas_call(
        functools.partial(
            expert_kernel, [(None,) * len(b) for b in blocks], [(None,) * len(t) for t in types]
        ),
        out_shape=shapes,
        in_specs=[VMEM] * (len(flat) + 2),
        out_specs=[VMEM] * len(shapes),
        cost_estimate=pl.CostEstimate(
            flops=int(work * FLOPS_US), bytes_accessed=0, transcendentals=0
        ),
        compiler_params=pltpu.CompilerParams(vmem_limit_bytes=16 * 1024 * 1024),
    )(*flat, *weights)


def part_kernel(index, both_ref, part_ref):
    part_ref[...] = both_ref[index]


def part_of(both, index):
    return pl.pallas_call(
        functools.partial(part_kernel, index),
        out_shape=jax.ShapeDtypeStruct(both.shape[1:], both.dtype),
        in_specs=[VMEM],
        out_specs=VMEM,
        cost_estimate=pl.CostEstimate(flops=int(FLOPS_US / 5), bytes_accessed=0, transcendentals=0),
        compiler_params=pltpu.CompilerParams(vmem_limit_bytes=4 * 1024 * 1024),
    )(both)


def cast_kernel(from_ref, to_ref):
    to_ref[...] = from_ref[...].astype(to_ref.dtype)


def cast(array, dtype, work):
    return pl.pallas_call(
        cast_kernel,
        out_shape=jax.ShapeDtypeStruct(array.shape, dtype),
        in_specs=[VMEM],
        out_specs=VMEM,
        cost_estimate=pl.CostEstimate(
            flops=int(work * FLOPS_US), bytes_accessed=0, transcendentals=0
        ),
        compiler_params=pltpu.CompilerParams(vmem_limit_bytes=4 * 1024 * 1024),
    )(array)


def add_kernel(one_ref, two_ref, out_ref):
    out_ref[...] = (one_ref[...] + two_ref[...].astype(jnp.float32)).astype(out_ref.dtype)


def add(one, two, work):
    return pl.pallas_call(
        add_kernel,
        out_shape=jax.ShapeDtypeStruct(two.shape, two.dtype),
        in_specs=[VMEM] * 2,
        out_specs=VMEM,
        cost_estimate=pl.CostEstimate(
            flops=int(work * FLOPS_US), bytes_accessed=0, transcendentals=0
        ),
        compiler_params=pltpu.CompilerParams(vmem_limit_bytes=4 * 1024 * 1024),
    )(one, two)


def pick_kernel(one_ref, two_ref, out_ref):
    first = lax.axis_index("tp") == 0

    @pl.when(first)
    def _():
        out_ref[...] = one_ref[...]

    @pl.when(jnp.logical_not(first))
    def _():
        out_ref[...] = two_ref[...]


def pick(one, two):
    return pl.pallas_call(
        pick_kernel,
        out_shape=jax.ShapeDtypeStruct(one.shape, one.dtype),
        in_specs=[VMEM] * 2,
        out_specs=VMEM,
        cost_estimate=pl.CostEstimate(flops=int(FLOPS_US / 5), bytes_accessed=0, transcendentals=0),
        compiler_params=pltpu.CompilerParams(vmem_limit_bytes=4 * 1024 * 1024),
    )(one, two)


def dense_body(tokens, expert_ids, gate_fixed, w_gate, w_up, w_down):
    tie = lax.optimization_barrier
    f32, bf16 = jnp.float32, jnp.bfloat16
    core = lax.axis_index("tp")
    first = core == 0
    half = tokens.shape[0] // 2
    top, bottom = tokens[:half], tokens[half:]
    a0, b0, place = tie(
        (jnp.where(first, top, bottom), jnp.where(first, bottom, top), lax.axis_index("ep"))
    )
    b0 = swap_core(b0)
    ours = pack(w_gate[0], w_up[0], w_down[0])

    def expert(blocks, types, work=1.0):
        return expert_block(blocks, weights, types, work)

    both0 = jnp.stack([a0, b0])
    z2a = swap(a0, 4)
    z2b = cast(swap(b0, 4), bf16, 0.3)
    z1 = swap(both0, 2)
    x0 = swap(both0, 1)
    z2a, ours = tie((z2a, ours))
    m6a = cast(swap(z2a, 2), bf16, 40.0)
    m5a = swap(z2a, 1)
    z2b, x0 = tie((z2b, x0))
    ours, z1 = tie((ours, z1))
    weights = [ours, swap_core(ours)]
    m5b = swap(z2b, 1)
    m6b = swap(z2b, 2)
    m5a, m6b = tie((m5a, m6b))
    m5b, held = tie((m5b, x0))
    m3 = swap(held, 2)
    m7a = swap(m6a, 1)
    m7b = swap(m5b, 2)
    p4, p5a, p5b = expert(((z2a, z2b), (m5a, m5b)), ((f32,), (bf16, f32)))
    m7a, m7b, p4, p5a, p5b = tie((m7a, m7b, p4, p5a, p5b))
    p6, p7a, p7b = expert(((m6a, m6b), (m7a, m7b)), ((f32,), (bf16, bf16)))
    p0, p1, p2, p3 = expert(
        ((both0,), (x0,), (z1,), (m3,)), ((f32,), (bf16,), (f32,), (bf16,)), 1.0
    )
    r7a = swap(p7a, 1)
    r7b = swap(p7b, 2)
    r7a, p1, p2, p3 = tie((r7a, p1, p2, p3))
    s6 = jnp.stack([p6[0] + r7a.astype(f32), p6[1]]).astype(bf16)
    r5a = cast(swap(p5a, 1), bf16, 2.0)
    s5b = add(p5b, r7b, 1.0)
    r6 = swap(s6, 2).astype(f32)
    r5b = swap(s5b, 1)
    r5 = jnp.stack([r5a, r5b]).astype(f32)
    sent = (p4 + r6 + r5).astype(bf16)
    s5b, p3 = tie((s5b, p3))
    r3 = swap(p3, 1)
    s2 = add(p2, r3, 0.1)
    sent, p1 = tie((sent, p1))
    other = cast(swap(sent, 4), f32, 0.5)
    r2 = swap(s2, 2)
    r1 = swap(p1, 1)
    near = p0 + r1.astype(f32) + r2.astype(f32)
    ids = jnp.where(first, expert_ids[:half], expert_ids[half:])
    scale = jnp.where(first, gate_fixed[:half], gate_fixed[half:]).astype(f32) / 2048.0
    offset = place - ids * ESPLIT
    here = (offset >= 0) & (offset < ESPLIT)
    mixed = jnp.where(here, near, other) * scale
    left, right = mixed[0].astype(bf16), mixed[1].astype(bf16)
    got = swap_core(right)
    return jnp.concatenate([jnp.where(first, left, got), jnp.where(first, got, left)], axis=0)


def routed_body(tokens, expert_ids, gate_fixed, w_gate, w_up, w_down):
    ep_count = lax.axis_size("ep")
    tok_dev, topk = expert_ids.shape
    experts = ep_count // ESPLIT
    capacity = max(2, min(tok_dev, 2 * tok_dev * topk // experts))
    flat_ids = expert_ids.reshape(-1)
    slot_index = flat_ids * capacity + earlier_ranks(flat_ids)
    chooser = (slot_index[None, :] == jnp.arange(experts * capacity)[:, None]).astype(jnp.bfloat16)
    whole = lax.all_gather(tokens, "tp", axis=1, tiled=True)
    width = whole.shape[1]
    routed_rows = jnp.repeat(whole, topk, axis=0)
    grouped = jnp.dot(chooser, routed_rows, preferred_element_type=jnp.float32).astype(jnp.bfloat16)
    grouped = grouped.reshape(experts, 1, capacity, width)
    copies = jnp.broadcast_to(grouped, (experts, ESPLIT, capacity, width))
    arrived = lax.all_to_all(
        copies.reshape(ep_count, capacity, width), "ep", split_axis=0, concat_axis=0, tiled=True
    )
    expert_rows = arrived.reshape(ep_count * capacity, arrived.shape[2])
    gate_act = jnp.dot(expert_rows, w_gate[0], preferred_element_type=jnp.float32)
    up_act = jnp.dot(expert_rows, w_up[0], preferred_element_type=jnp.float32)
    hidden = (jax.nn.silu(gate_act) * up_act).astype(jnp.bfloat16)
    partial_out = jnp.dot(hidden, w_down[0], preferred_element_type=jnp.float32).astype(
        jnp.bfloat16
    )
    summed = (
        lax.psum_scatter(partial_out, "tp", scatter_dimension=1, tiled=True)
        .astype(jnp.float32)
        .astype(jnp.bfloat16)
    )
    returned = lax.all_to_all(
        summed.reshape(ep_count, capacity, summed.shape[1]),
        "ep",
        split_axis=0,
        concat_axis=0,
        tiled=True,
    )
    quarters = jnp.sum(
        returned.reshape(experts, ESPLIT, capacity, returned.shape[2]).astype(jnp.float32), axis=1
    )
    quarters = quarters.reshape(experts * capacity, returned.shape[2])
    weights_route = gate_fixed.reshape(-1).astype(jnp.float32) / 2048.0
    routed = quarters[slot_index] * weights_route[:, None]
    return jnp.sum(routed.reshape(tok_dev, topk, routed.shape[1]), axis=1).astype(jnp.bfloat16)


def body(tokens, expert_ids, *rest):
    experts = lax.axis_size("ep") // ESPLIT
    dense = experts == 2 and expert_ids.shape[1] == 1
    return (dense_body if dense else routed_body)(tokens, expert_ids, *rest)


def solution(mesh):
    placed = (
        P(("groups", "ep"), "tp"),
        P(("groups", "ep"), None),
        P(("groups", "ep"), None),
        P("ep", None, "tp"),
        P("ep", None, "tp"),
        P("ep", "tp", None),
    )
    return jax.shard_map(
        body, mesh=mesh, in_specs=placed, out_specs=P(("groups", "ep"), "tp"), check_vma=False
    )
```

```python
import functools

import jax
import jax.numpy as jnp
from jax import lax
from jax.experimental import pallas as pl
from jax.experimental.pallas import tpu as pltpu
from jax.sharding import PartitionSpec as P

ESPLIT = 4
FLOPS_US = 1.15e9
VMEM = pl.BlockSpec(memory_space=pltpu.VMEM)


def earlier_ranks(labels):
    position = jnp.arange(labels.shape[0])
    matches = (labels[:, None] == labels[None, :]) & (position[:, None] < position[None, :])
    return jnp.sum(matches, axis=0)


def swap(value, bit):
    pairs = [(i, i ^ bit) for i in range(lax.axis_size("ep"))]
    return lax.ppermute(value, "ep", pairs)


def swap_of(value, bit, core):
    pairs = [(2 * i + core, 2 * (i ^ bit) + core) for i in range(lax.axis_size("ep"))]
    return lax.ppermute(value, ("ep", "tp"), pairs)


def swap_core(value):
    return lax.ppermute(value, "tp", [(0, 1), (1, 0)])


def pack_kernel(gate_ref, up_ref, down_ref, pack_ref, sems):
    depth, units = gate_ref.shape
    pairs = [(gate_ref, pack_ref.at[:, :units]), (up_ref, pack_ref.at[:, units : 2 * units])]
    for at in range(0, depth, units):
        pairs.append((down_ref.at[:, at : at + units], pack_ref.at[at : at + units, 2 * units :]))
    copies = [pltpu.make_async_copy(*pair, sems.at[i]) for i, pair in enumerate(pairs)]
    for copy in copies:
        copy.start()
    for copy in copies:
        copy.wait()


def pack(gate, up, down):
    depth, units = gate.shape
    return pl.pallas_call(
        pack_kernel,
        out_shape=jax.ShapeDtypeStruct((depth, 3 * units), gate.dtype),
        in_specs=[pl.BlockSpec(memory_space=pl.ANY)] * 3,
        out_specs=VMEM,
        scratch_shapes=[pltpu.SemaphoreType.DMA((2 + depth // units,))],
        cost_estimate=pl.CostEstimate(flops=int(2 * FLOPS_US), bytes_accessed=0, transcendentals=0),
        compiler_params=pltpu.CompilerParams(vmem_limit_bytes=8 * 1024 * 1024),
    )(gate, up, down)


def expert_kernel(blocks_in, blocks_out, *refs):
    def take(shape):
        nonlocal refs
        taken, refs = refs[: len(shape)], refs[len(shape) :]
        return taken

    def parts(held):
        return held if len(held) == 2 else (held[0].at[0], held[0].at[1])

    blocks = [parts(take(block)) for block in blocks_in]
    packs = take((None, None))
    sums = [parts(take(block)) for block in blocks_out]
    rows, width = blocks[0][0].shape
    first = lax.axis_index("tp") == 0

    def run(order):
        whole = jnp.concatenate(
            [jnp.concatenate([block[i][...] for block in blocks], axis=0) for i in order], axis=1
        )
        out = None
        for held in packs:
            depth, units = held.shape[0], held.shape[1] // 3
            act = jnp.dot(whole, held[:, : 2 * units], preferred_element_type=jnp.float32)
            w_out = jnp.concatenate(
                [held[at : at + units, 2 * units :] for at in range(0, depth, units)], axis=1
            )
            gate, up = act[:, :units], act[:, units:]
            hidden = (gate / (1 + jnp.exp(-gate)) * up).astype(jnp.bfloat16)
            part = jnp.dot(hidden, w_out, preferred_element_type=jnp.float32)
            out = part if out is None else out + part
        for place, i in enumerate(order):
            for j, held in enumerate(sums):
                part = out[j * rows : (j + 1) * rows, place * width : (place + 1) * width]
                held[i][...] = part.astype(held[i].dtype)

    @pl.when(first)
    def _():
        run((0, 1))

    @pl.when(jnp.logical_not(first))
    def _():
        run((1, 0))


def expert_block(blocks, weights, types, work):
    half, width = blocks[0][0].shape[-2:]
    shapes = [
        jax.ShapeDtypeStruct((half, width) if len(pair) == 2 else (2, half, width), t)
        for pair in types
        for t in pair
    ]
    flat = [array for block in blocks for array in block]
    return pl.pallas_call(
        functools.partial(
            expert_kernel, [(None,) * len(b) for b in blocks], [(None,) * len(t) for t in types]
        ),
        out_shape=shapes,
        in_specs=[VMEM] * (len(flat) + 2),
        out_specs=[VMEM] * len(shapes),
        cost_estimate=pl.CostEstimate(
            flops=int(work * FLOPS_US), bytes_accessed=0, transcendentals=0
        ),
        compiler_params=pltpu.CompilerParams(vmem_limit_bytes=16 * 1024 * 1024),
    )(*flat, *weights)


def part_kernel(index, both_ref, part_ref):
    part_ref[...] = both_ref[index]


def part_of(both, index):
    return pl.pallas_call(
        functools.partial(part_kernel, index),
        out_shape=jax.ShapeDtypeStruct(both.shape[1:], both.dtype),
        in_specs=[VMEM],
        out_specs=VMEM,
        cost_estimate=pl.CostEstimate(flops=int(FLOPS_US / 5), bytes_accessed=0, transcendentals=0),
        compiler_params=pltpu.CompilerParams(vmem_limit_bytes=4 * 1024 * 1024),
    )(both)


def cast_kernel(from_ref, to_ref):
    to_ref[...] = from_ref[...].astype(to_ref.dtype)


def cast(array, dtype, work):
    return pl.pallas_call(
        cast_kernel,
        out_shape=jax.ShapeDtypeStruct(array.shape, dtype),
        in_specs=[VMEM],
        out_specs=VMEM,
        cost_estimate=pl.CostEstimate(
            flops=int(work * FLOPS_US), bytes_accessed=0, transcendentals=0
        ),
        compiler_params=pltpu.CompilerParams(vmem_limit_bytes=4 * 1024 * 1024),
    )(array)


def add_kernel(one_ref, two_ref, out_ref):
    out_ref[...] = (one_ref[...] + two_ref[...].astype(jnp.float32)).astype(out_ref.dtype)


def add(one, two, work):
    return pl.pallas_call(
        add_kernel,
        out_shape=jax.ShapeDtypeStruct(two.shape, two.dtype),
        in_specs=[VMEM] * 2,
        out_specs=VMEM,
        cost_estimate=pl.CostEstimate(
            flops=int(work * FLOPS_US), bytes_accessed=0, transcendentals=0
        ),
        compiler_params=pltpu.CompilerParams(vmem_limit_bytes=4 * 1024 * 1024),
    )(one, two)


def pick_kernel(one_ref, two_ref, out_ref):
    first = lax.axis_index("tp") == 0

    @pl.when(first)
    def _():
        out_ref[...] = one_ref[...]

    @pl.when(jnp.logical_not(first))
    def _():
        out_ref[...] = two_ref[...]


def pick(one, two):
    return pl.pallas_call(
        pick_kernel,
        out_shape=jax.ShapeDtypeStruct(one.shape, one.dtype),
        in_specs=[VMEM] * 2,
        out_specs=VMEM,
        cost_estimate=pl.CostEstimate(flops=int(FLOPS_US / 5), bytes_accessed=0, transcendentals=0),
        compiler_params=pltpu.CompilerParams(vmem_limit_bytes=4 * 1024 * 1024),
    )(one, two)


def dense_body(tokens, expert_ids, gate_fixed, w_gate, w_up, w_down):
    tie = lax.optimization_barrier
    f32, bf16 = jnp.float32, jnp.bfloat16
    core = lax.axis_index("tp")
    first = core == 0
    half = tokens.shape[0] // 2
    top, bottom = tokens[:half], tokens[half:]
    a0, b0, place = tie(
        (jnp.where(first, top, bottom), jnp.where(first, bottom, top), lax.axis_index("ep"))
    )
    b0 = swap_core(b0)
    ours = pack(w_gate[0], w_up[0], w_down[0])

    def expert(blocks, types, work=1.0):
        return expert_block(blocks, weights, types, work)

    both0 = jnp.stack([a0, b0])
    z2a = swap(a0, 4)
    z2b = swap(b0, 4)
    z1 = swap(both0, 2)
    x0 = swap(both0, 1)
    z2a, ours = tie((z2a, ours))
    m6a = cast(swap(z2a, 2), bf16, 40.0)
    m5a = swap(z2a, 1)
    z2b, x0 = tie((z2b, x0))
    ours, z1 = tie((ours, z1))
    weights = [ours, swap_core(ours)]
    m5b = swap(z2b, 1)
    m6b = swap(z2b, 2)
    m5a, m6b = tie((m5a, m6b))
    m5b, held = tie((m5b, x0))
    m3 = swap(held, 2)
    m7a = swap(m6a, 1)
    m7b = swap(m5b, 2)
    p4, p5a, p5b = expert(((z2a, z2b), (m5a, m5b)), ((f32,), (bf16, f32)), 0.3)
    m7a, m7b, p4, p5a, p5b = tie((m7a, m7b, p4, p5a, p5b))
    p6, p7a, p7b = expert(((m6a, m6b), (m7a, m7b)), ((f32,), (bf16, bf16)))
    p0, p1, p2, p3 = expert(
        ((both0,), (x0,), (z1,), (m3,)), ((f32,), (bf16,), (f32,), (bf16,)), 1.0
    )
    r7a = swap(p7a, 1)
    r7b = swap(p7b, 2)
    r7a, p1, p2, p3 = tie((r7a, p1, p2, p3))
    s6 = jnp.stack([p6[0] + r7a.astype(f32), p6[1]]).astype(bf16)
    r5a = cast(swap(p5a, 1), bf16, 2.0)
    s5b = add(p5b, r7b, 1.0)
    r6 = swap(s6, 2).astype(f32)
    r5b = swap(s5b, 1)
    r5 = jnp.stack([r5a, r5b]).astype(f32)
    sent = (p4 + r6 + r5).astype(bf16)
    s5b, p3 = tie((s5b, p3))
    r3 = swap(p3, 1)
    s2 = add(p2, r3, 0.1)
    sent, p1 = tie((sent, p1))
    other = cast(swap(sent, 4), f32, 0.5)
    r2 = swap(s2, 2)
    r1 = swap(p1, 1)
    near = p0 + r1.astype(f32) + r2.astype(f32)
    ids = jnp.where(first, expert_ids[:half], expert_ids[half:])
    scale = jnp.where(first, gate_fixed[:half], gate_fixed[half:]).astype(f32) / 2048.0
    offset = place - ids * ESPLIT
    here = (offset >= 0) & (offset < ESPLIT)
    mixed = jnp.where(here, near, other) * scale
    left, right = mixed[0].astype(bf16), mixed[1].astype(bf16)
    got = swap_core(right)
    return jnp.concatenate([jnp.where(first, left, got), jnp.where(first, got, left)], axis=0)


def routed_body(tokens, expert_ids, gate_fixed, w_gate, w_up, w_down):
    ep_count = lax.axis_size("ep")
    tok_dev, topk = expert_ids.shape
    experts = ep_count // ESPLIT
    capacity = max(2, min(tok_dev, 2 * tok_dev * topk // experts))
    flat_ids = expert_ids.reshape(-1)
    slot_index = flat_ids * capacity + earlier_ranks(flat_ids)
    chooser = (slot_index[None, :] == jnp.arange(experts * capacity)[:, None]).astype(jnp.bfloat16)
    whole = lax.all_gather(tokens, "tp", axis=1, tiled=True)
    width = whole.shape[1]
    routed_rows = jnp.repeat(whole, topk, axis=0)
    grouped = jnp.dot(chooser, routed_rows, preferred_element_type=jnp.float32).astype(jnp.bfloat16)
    grouped = grouped.reshape(experts, 1, capacity, width)
    copies = jnp.broadcast_to(grouped, (experts, ESPLIT, capacity, width))
    arrived = lax.all_to_all(
        copies.reshape(ep_count, capacity, width), "ep", split_axis=0, concat_axis=0, tiled=True
    )
    expert_rows = arrived.reshape(ep_count * capacity, arrived.shape[2])
    gate_act = jnp.dot(expert_rows, w_gate[0], preferred_element_type=jnp.float32)
    up_act = jnp.dot(expert_rows, w_up[0], preferred_element_type=jnp.float32)
    hidden = (jax.nn.silu(gate_act) * up_act).astype(jnp.bfloat16)
    partial_out = jnp.dot(hidden, w_down[0], preferred_element_type=jnp.float32).astype(
        jnp.bfloat16
    )
    summed = (
        lax.psum_scatter(partial_out, "tp", scatter_dimension=1, tiled=True)
        .astype(jnp.float32)
        .astype(jnp.bfloat16)
    )
    returned = lax.all_to_all(
        summed.reshape(ep_count, capacity, summed.shape[1]),
        "ep",
        split_axis=0,
        concat_axis=0,
        tiled=True,
    )
    quarters = jnp.sum(
        returned.reshape(experts, ESPLIT, capacity, returned.shape[2]).astype(jnp.float32), axis=1
    )
    quarters = quarters.reshape(experts * capacity, returned.shape[2])
    weights_route = gate_fixed.reshape(-1).astype(jnp.float32) / 2048.0
    routed = quarters[slot_index] * weights_route[:, None]
    return jnp.sum(routed.reshape(tok_dev, topk, routed.shape[1]), axis=1).astype(jnp.bfloat16)


def body(tokens, expert_ids, *rest):
    experts = lax.axis_size("ep") // ESPLIT
    dense = experts == 2 and expert_ids.shape[1] == 1
    return (dense_body if dense else routed_body)(tokens, expert_ids, *rest)


def solution(mesh):
    placed = (
        P(("groups", "ep"), "tp"),
        P(("groups", "ep"), None),
        P(("groups", "ep"), None),
        P("ep", None, "tp"),
        P("ep", None, "tp"),
        P("ep", "tp", None),
    )
    return jax.shard_map(
        body, mesh=mesh, in_specs=placed, out_specs=P(("groups", "ep"), "tp"), check_vma=False
    )
```

```python
import functools

import jax
import jax.numpy as jnp
from jax import lax
from jax.experimental import pallas as pl
from jax.experimental.pallas import tpu as pltpu
from jax.sharding import PartitionSpec as P

ESPLIT = 4
FLOPS_US = 1.15e9
VMEM = pl.BlockSpec(memory_space=pltpu.VMEM)


def earlier_ranks(labels):
    position = jnp.arange(labels.shape[0])
    matches = (labels[:, None] == labels[None, :]) & (position[:, None] < position[None, :])
    return jnp.sum(matches, axis=0)


def swap(value, bit):
    pairs = [(i, i ^ bit) for i in range(lax.axis_size("ep"))]
    return lax.ppermute(value, "ep", pairs)


def swap_of(value, bit, core):
    pairs = [(2 * i + core, 2 * (i ^ bit) + core) for i in range(lax.axis_size("ep"))]
    return lax.ppermute(value, ("ep", "tp"), pairs)


def swap_core(value):
    return lax.ppermute(value, "tp", [(0, 1), (1, 0)])


def pack_kernel(gate_ref, up_ref, down_ref, pack_ref, sems):
    depth, units = gate_ref.shape
    pairs = [(gate_ref, pack_ref.at[:, :units]), (up_ref, pack_ref.at[:, units : 2 * units])]
    for at in range(0, depth, units):
        pairs.append((down_ref.at[:, at : at + units], pack_ref.at[at : at + units, 2 * units :]))
    copies = [pltpu.make_async_copy(*pair, sems.at[i]) for i, pair in enumerate(pairs)]
    for copy in copies:
        copy.start()
    for copy in copies:
        copy.wait()


def pack(gate, up, down):
    depth, units = gate.shape
    return pl.pallas_call(
        pack_kernel,
        out_shape=jax.ShapeDtypeStruct((depth, 3 * units), gate.dtype),
        in_specs=[pl.BlockSpec(memory_space=pl.ANY)] * 3,
        out_specs=VMEM,
        scratch_shapes=[pltpu.SemaphoreType.DMA((2 + depth // units,))],
        cost_estimate=pl.CostEstimate(flops=int(2 * FLOPS_US), bytes_accessed=0, transcendentals=0),
        compiler_params=pltpu.CompilerParams(vmem_limit_bytes=8 * 1024 * 1024),
    )(gate, up, down)


def expert_kernel(blocks_in, blocks_out, *refs):
    def take(shape):
        nonlocal refs
        taken, refs = refs[: len(shape)], refs[len(shape) :]
        return taken

    def parts(held):
        return held if len(held) == 2 else (held[0].at[0], held[0].at[1])

    blocks = [parts(take(block)) for block in blocks_in]
    packs = take((None, None))
    sums = [parts(take(block)) for block in blocks_out]
    rows, width = blocks[0][0].shape
    first = lax.axis_index("tp") == 0

    def run(order):
        whole = jnp.concatenate(
            [jnp.concatenate([block[i][...] for block in blocks], axis=0) for i in order], axis=1
        )
        out = None
        for held in packs:
            depth, units = held.shape[0], held.shape[1] // 3
            act = jnp.dot(whole, held[:, : 2 * units], preferred_element_type=jnp.float32)
            w_out = jnp.concatenate(
                [held[at : at + units, 2 * units :] for at in range(0, depth, units)], axis=1
            )
            gate, up = act[:, :units], act[:, units:]
            hidden = (gate / (1 + jnp.exp(-gate)) * up).astype(jnp.bfloat16)
            part = jnp.dot(hidden, w_out, preferred_element_type=jnp.float32)
            out = part if out is None else out + part
        for place, i in enumerate(order):
            for j, held in enumerate(sums):
                part = out[j * rows : (j + 1) * rows, place * width : (place + 1) * width]
                held[i][...] = part.astype(held[i].dtype)

    @pl.when(first)
    def _():
        run((0, 1))

    @pl.when(jnp.logical_not(first))
    def _():
        run((1, 0))


def expert_block(blocks, weights, types, work):
    half, width = blocks[0][0].shape[-2:]
    shapes = [
        jax.ShapeDtypeStruct((half, width) if len(pair) == 2 else (2, half, width), t)
        for pair in types
        for t in pair
    ]
    flat = [array for block in blocks for array in block]
    return pl.pallas_call(
        functools.partial(
            expert_kernel, [(None,) * len(b) for b in blocks], [(None,) * len(t) for t in types]
        ),
        out_shape=shapes,
        in_specs=[VMEM] * (len(flat) + 2),
        out_specs=[VMEM] * len(shapes),
        cost_estimate=pl.CostEstimate(
            flops=int(work * FLOPS_US), bytes_accessed=0, transcendentals=0
        ),
        compiler_params=pltpu.CompilerParams(vmem_limit_bytes=16 * 1024 * 1024),
    )(*flat, *weights)


def part_kernel(index, both_ref, part_ref):
    part_ref[...] = both_ref[index]


def part_of(both, index):
    return pl.pallas_call(
        functools.partial(part_kernel, index),
        out_shape=jax.ShapeDtypeStruct(both.shape[1:], both.dtype),
        in_specs=[VMEM],
        out_specs=VMEM,
        cost_estimate=pl.CostEstimate(flops=int(FLOPS_US / 5), bytes_accessed=0, transcendentals=0),
        compiler_params=pltpu.CompilerParams(vmem_limit_bytes=4 * 1024 * 1024),
    )(both)


def cast_kernel(from_ref, to_ref):
    to_ref[...] = from_ref[...].astype(to_ref.dtype)


def cast(array, dtype, work):
    return pl.pallas_call(
        cast_kernel,
        out_shape=jax.ShapeDtypeStruct(array.shape, dtype),
        in_specs=[VMEM],
        out_specs=VMEM,
        cost_estimate=pl.CostEstimate(
            flops=int(work * FLOPS_US), bytes_accessed=0, transcendentals=0
        ),
        compiler_params=pltpu.CompilerParams(vmem_limit_bytes=4 * 1024 * 1024),
    )(array)


def add_kernel(one_ref, two_ref, out_ref):
    out_ref[...] = (one_ref[...] + two_ref[...].astype(jnp.float32)).astype(out_ref.dtype)


def add(one, two, work):
    return pl.pallas_call(
        add_kernel,
        out_shape=jax.ShapeDtypeStruct(two.shape, two.dtype),
        in_specs=[VMEM] * 2,
        out_specs=VMEM,
        cost_estimate=pl.CostEstimate(
            flops=int(work * FLOPS_US), bytes_accessed=0, transcendentals=0
        ),
        compiler_params=pltpu.CompilerParams(vmem_limit_bytes=4 * 1024 * 1024),
    )(one, two)


def pick_kernel(one_ref, two_ref, out_ref):
    first = lax.axis_index("tp") == 0

    @pl.when(first)
    def _():
        out_ref[...] = one_ref[...]

    @pl.when(jnp.logical_not(first))
    def _():
        out_ref[...] = two_ref[...]


def pick(one, two):
    return pl.pallas_call(
        pick_kernel,
        out_shape=jax.ShapeDtypeStruct(one.shape, one.dtype),
        in_specs=[VMEM] * 2,
        out_specs=VMEM,
        cost_estimate=pl.CostEstimate(flops=int(FLOPS_US / 5), bytes_accessed=0, transcendentals=0),
        compiler_params=pltpu.CompilerParams(vmem_limit_bytes=4 * 1024 * 1024),
    )(one, two)


def dense_body(tokens, expert_ids, gate_fixed, w_gate, w_up, w_down):
    tie = lax.optimization_barrier
    f32, bf16 = jnp.float32, jnp.bfloat16
    core = lax.axis_index("tp")
    first = core == 0
    half = tokens.shape[0] // 2
    top, bottom = tokens[:half], tokens[half:]
    a0, b0, place = tie(
        (jnp.where(first, top, bottom), jnp.where(first, bottom, top), lax.axis_index("ep"))
    )
    b0 = swap_core(b0)
    ours = pack(w_gate[0], w_up[0], w_down[0])

    def expert(blocks, types, work=1.0):
        return expert_block(blocks, weights, types, work)

    both0 = jnp.stack([a0, b0])
    z2a = swap(a0, 4)
    z2b = swap(b0, 4)
    z1 = swap(both0, 2)
    x0 = swap(both0, 1)
    z2a, ours = tie((z2a, ours))
    m6a = cast(swap(z2a, 2), bf16, 40.0)
    m5a = swap(z2a, 1)
    z2b, x0 = tie((z2b, x0))
    ours, z1 = tie((ours, z1))
    weights = [ours, swap_core(ours)]
    m5b = swap(z2b, 1)
    m6b = swap(z2b, 2)
    m5a, m6b = tie((m5a, m6b))
    m5b, held = tie((m5b, x0))
    m3 = swap(held, 2)
    m7a = swap(m6a, 1)
    m7b = swap(m5b, 2)
    p4, p5a, p5b = expert(((z2a, z2b), (m5a, m5b)), ((f32,), (bf16, f32)), 0.3)
    m7a, m7b, p4, p5a, p5b = tie((m7a, m7b, p4, p5a, p5b))
    p6, p7a, p7b = expert(((m6a, m6b), (m7a, m7b)), ((f32,), (bf16, bf16)))
    p0, p1, p2, p3 = expert(
        ((both0,), (x0,), (z1,), (m3,)), ((f32,), (bf16,), (f32,), (bf16,)), 1.0
    )
    r7a = swap(p7a, 1)
    r7b = swap(p7b, 2)
    r7a, p1, p2, p3 = tie((r7a, p1, p2, p3))
    s6 = jnp.stack([p6[0] + r7a.astype(f32), p6[1]]).astype(bf16)
    r5a = cast(swap(p5a, 1), bf16, 2.0)
    s5b = add(p5b, r7b, 1.0)
    r6 = swap(s6, 2).astype(f32)
    r5b = swap(s5b, 1)
    r5 = jnp.stack([r5a, r5b]).astype(f32)
    sent = (p4 + r6 + r5).astype(bf16)
    s5b, p3 = tie((s5b, p3))
    r3 = swap(p3, 1)
    s2 = add(p2, r3, 0.1)
    sent, p1 = tie((sent, p1))
    other = cast(swap(sent, 4), bf16, 0.5).astype(f32)
    r2 = swap(s2, 2)
    r1 = swap(p1, 1)
    near = p0 + r1.astype(f32) + r2.astype(f32)
    ids = jnp.where(first, expert_ids[:half], expert_ids[half:])
    scale = jnp.where(first, gate_fixed[:half], gate_fixed[half:]).astype(f32) / 2048.0
    offset = place - ids * ESPLIT
    here = (offset >= 0) & (offset < ESPLIT)
    mixed = jnp.where(here, near, other) * scale
    left, right = mixed[0].astype(bf16), mixed[1].astype(bf16)
    got = swap_core(right)
    return jnp.concatenate([jnp.where(first, left, got), jnp.where(first, got, left)], axis=0)


def routed_body(tokens, expert_ids, gate_fixed, w_gate, w_up, w_down):
    ep_count = lax.axis_size("ep")
    tok_dev, topk = expert_ids.shape
    experts = ep_count // ESPLIT
    capacity = max(2, min(tok_dev, 2 * tok_dev * topk // experts))
    flat_ids = expert_ids.reshape(-1)
    slot_index = flat_ids * capacity + earlier_ranks(flat_ids)
    chooser = (slot_index[None, :] == jnp.arange(experts * capacity)[:, None]).astype(jnp.bfloat16)
    whole = lax.all_gather(tokens, "tp", axis=1, tiled=True)
    width = whole.shape[1]
    routed_rows = jnp.repeat(whole, topk, axis=0)
    grouped = jnp.dot(chooser, routed_rows, preferred_element_type=jnp.float32).astype(jnp.bfloat16)
    grouped = grouped.reshape(experts, 1, capacity, width)
    copies = jnp.broadcast_to(grouped, (experts, ESPLIT, capacity, width))
    arrived = lax.all_to_all(
        copies.reshape(ep_count, capacity, width), "ep", split_axis=0, concat_axis=0, tiled=True
    )
    expert_rows = arrived.reshape(ep_count * capacity, arrived.shape[2])
    gate_act = jnp.dot(expert_rows, w_gate[0], preferred_element_type=jnp.float32)
    up_act = jnp.dot(expert_rows, w_up[0], preferred_element_type=jnp.float32)
    hidden = (jax.nn.silu(gate_act) * up_act).astype(jnp.bfloat16)
    partial_out = jnp.dot(hidden, w_down[0], preferred_element_type=jnp.float32).astype(
        jnp.bfloat16
    )
    summed = (
        lax.psum_scatter(partial_out, "tp", scatter_dimension=1, tiled=True)
        .astype(jnp.float32)
        .astype(jnp.bfloat16)
    )
    returned = lax.all_to_all(
        summed.reshape(ep_count, capacity, summed.shape[1]),
        "ep",
        split_axis=0,
        concat_axis=0,
        tiled=True,
    )
    quarters = jnp.sum(
        returned.reshape(experts, ESPLIT, capacity, returned.shape[2]).astype(jnp.float32), axis=1
    )
    quarters = quarters.reshape(experts * capacity, returned.shape[2])
    weights_route = gate_fixed.reshape(-1).astype(jnp.float32) / 2048.0
    routed = quarters[slot_index] * weights_route[:, None]
    return jnp.sum(routed.reshape(tok_dev, topk, routed.shape[1]), axis=1).astype(jnp.bfloat16)


def body(tokens, expert_ids, *rest):
    experts = lax.axis_size("ep") // ESPLIT
    dense = experts == 2 and expert_ids.shape[1] == 1
    return (dense_body if dense else routed_body)(tokens, expert_ids, *rest)


def solution(mesh):
    placed = (
        P(("groups", "ep"), "tp"),
        P(("groups", "ep"), None),
        P(("groups", "ep"), None),
        P("ep", None, "tp"),
        P("ep", None, "tp"),
        P("ep", "tp", None),
    )
    return jax.shard_map(
        body, mesh=mesh, in_specs=placed, out_specs=P(("groups", "ep"), "tp"), check_vma=False
    )
```
